256 devices in a mesh: dp: 64 (over y_lo, x, z), grp: 4 (over y_hi, core).
Axes of the slice: x: 4, y: 4 (y_hi: 2, y_lo: 2; y = y_hi * 2 + y_lo), z: 8, core: 2. Of those that a mesh axis runs over, the one named last changes fastest.
Arguments:
- acts: bfloat16 [4, 32768, 4096], P('grp', 'dp'), may hold values from -110 to 110
- out_grads: bfloat16 [4, 32768, 4096], P('grp', 'dp'), may hold values from -110 to 110
- proj_in: int32 [4, 64, 4096], P('grp'), may hold values from 0 to 1
- proj_out: int32 [4, 64, 4096], P('grp'), may hold values from 0 to 1
- query_grads: bfloat16 [4, 2048, 4096], P('grp', 'dp'), may hold values from -0.4375 to 0.4375
Outputs:
- scores: float32 [2048, 512], P('grp', 'dp')
The draws below stay inside these ranges and needn't reach their ends.
All inputs are finite; a program needn't handle non-finite values.
Results may differ from the reference program's by a relative error of at most 0.015.
The reference program's roundings to bfloat16 on the way (of `train_grads` and `whitened`) count: a program that leaves them out, or rounds other values in their place, can miss the bound.
Values may be sent and summed in bfloat16 or wider, within the bound.
No kernel may reach another device: no remote copies, remote signals or barrier semaphores. Data moves between devices by JAX's collectives and lax.ppermute only.
A program may use at most 128 MiB of HBM per device.

```python
import math
import jax
import jax.numpy as jnp
from jax import lax

D = 4096
RANK = 64
SEQ = 64
PROJ = 4096
LAYERS = 4
TOKENS = 32768
QUERIES = 2048


def shape_field(key, base_noise, mix_weight, period):
    latent_key, scale_key = jax.random.split(key)
    latent = jnp.clip(jax.random.normal(latent_key, (LAYERS, TOKENS, period), jnp.float32), -4.0, 4.0)
    shared = jnp.tile(latent, (1, 1, D // period))
    position = jnp.arange(TOKENS, dtype=jnp.float32) / TOKENS
    tok_scale = jnp.exp(jax.random.uniform(scale_key, (LAYERS, TOKENS, 1), jnp.float32, 0.0, math.log(3.0)))
    tok_scale = tok_scale * (1.0 + 2.0 * position)[None, :, None]
    return tok_scale * (base_noise + mix_weight * shared)


def draw_acts(key, part):
    key = jax.random.fold_in(key, 11)
    noise_key, rest_key = jax.random.split(key)
    base_noise = jnp.clip(jax.random.normal(noise_key, (LAYERS, TOKENS, D), jnp.float32), -4.0, 4.0)
    return shape_field(rest_key, base_noise, 2.0, 16).astype(jnp.bfloat16)


def draw_out_grads(key, part):
    key = jax.random.fold_in(key, 12)
    noise_key, rest_key = jax.random.split(key)
    base_noise = jnp.clip(jax.random.normal(noise_key, (LAYERS, TOKENS, D), jnp.float32), -4.0, 4.0)
    return shape_field(rest_key, base_noise, 2.0, 8).astype(jnp.bfloat16)


def plant(values, rng, smallest, largest):
    longest = values.shape.index(max(values.shape))
    spots = []
    for shift in (0, 1):
        where = [jax.random.randint(jax.random.fold_in(rng, axis), (), 0, length) for axis, length in enumerate(values.shape)]
        where[longest] = (where[longest] + shift) % values.shape[longest]
        spots.append(tuple(where))
    return values.at[spots[0]].set(smallest).at[spots[1]].set(largest)


def shard_levels(own_key, dims, shards, low, high):
    def one(axis_at, parts):
        steps = jax.random.uniform(jax.random.fold_in(jax.random.fold_in(own_key, 6), axis_at), (parts,), jnp.float32, low / len(shards), high / len(shards))
        return jnp.repeat(jnp.exp(steps), dims[axis_at] // parts).reshape((-1,) + (1,) * (len(dims) - axis_at - 1))

    level = one(*shards[0])
    for cut in shards[1:]:
        level = level * one(*cut)
    return level


def bell_draw(key, shape, spread, limit, shards=(), held_as=jnp.bfloat16):
    result = spread * jax.random.normal(key, shape, jnp.float32)
    if shards:
        result = result * shard_levels(key, shape, shards, -0.22, 0.18)
    return jnp.clip(result, -limit, limit).astype(held_as)


def setup_inputs(seed: int = 0) -> dict:
    key_of = jax.random.split(jax.random.key(seed), 6)
    return {
        "acts": draw_acts(jax.random.fold_in(key_of[5], 71), 0),
        "out_grads": draw_out_grads(jax.random.fold_in(key_of[5], 71), 0),
        "proj_in": plant(jax.random.randint(key_of[2], (LAYERS, RANK, D), 0, 2), jax.random.fold_in(key_of[2], 1), 0, 1).astype(jnp.int32),
        "proj_out": plant(jax.random.randint(key_of[3], (LAYERS, RANK, D), 0, 2), jax.random.fold_in(key_of[3], 1), 0, 1).astype(jnp.int32),
        "query_grads": bell_draw(key_of[4], (LAYERS, QUERIES, PROJ), 0.03, 0.4375, ((0, 4), (1, 64))),
    }


DAMPING = 0.1
HIGH = lax.Precision.HIGHEST

def sign_matrix(table, feat_width):
    return ((2 * table - 1).astype(jnp.float32) * (1.0 / math.sqrt(feat_width))).astype(jnp.bfloat16)

def project_rows(values, matrix):
    return lax.dot_general(values.astype(jnp.float32), matrix.astype(jnp.float32), (((1,), (1,)), ((), ())), preferred_element_type=jnp.float32)

def damped_inverse(factor):
    proj_rank = factor.shape[0]
    identity = jnp.eye(proj_rank, dtype=factor.dtype)
    ridge_term = DAMPING * jnp.trace(factor) / proj_rank
    chol_lower = jnp.linalg.cholesky(factor + ridge_term * identity)
    return jax.scipy.linalg.cho_solve((chol_lower, True), identity)

def per_example(x_proj, g_proj, proj_rank):
    x_blocks = x_proj.reshape(-1, SEQ, proj_rank)
    g_blocks = g_proj.reshape(-1, SEQ, proj_rank)
    outer = jnp.einsum('eto,eti->eoi', g_blocks, x_blocks, precision=HIGH)
    return outer.reshape(-1, proj_rank * proj_rank).astype(jnp.bfloat16)

def whiten_blocks(queries, inv_in, inv_out, proj_rank):
    square_blocks = queries.astype(jnp.float32).reshape(-1, proj_rank, proj_rank)
    left_mult = jnp.einsum('ab,nbc->nac', inv_out, square_blocks, precision=HIGH)
    both_sides = jnp.einsum('nac,cd->nad', left_mult, inv_in, precision=HIGH)
    return both_sides.reshape(-1, proj_rank * proj_rank).astype(jnp.bfloat16)

def score_block(left_rows, right_rows):
    return lax.dot_general(left_rows.astype(jnp.float32), right_rows.astype(jnp.float32), (((1,), (1,)), ((), ())), preferred_element_type=jnp.float32)

def reference(acts, out_grads, proj_in, proj_out, query_grads):
    layer_count, token_count, feat_width = acts.shape
    proj_rank = proj_in.shape[1]
    running = jnp.zeros((query_grads.shape[1], token_count // SEQ), jnp.float32)
    for layer_idx in range(layer_count):
        p_in = sign_matrix(proj_in[layer_idx], feat_width)
        p_out = sign_matrix(proj_out[layer_idx], feat_width)
        x_proj = project_rows(acts[layer_idx], p_in)
        g_proj = project_rows(out_grads[layer_idx], p_out)
        factor_in = jnp.dot(x_proj.T, x_proj, precision=HIGH) / token_count
        factor_out = jnp.dot(g_proj.T, g_proj, precision=HIGH) / token_count
        inv_in = damped_inverse(factor_in)
        inv_out = damped_inverse(factor_out)
        train_grads = per_example(x_proj, g_proj, proj_rank)
        whitened = whiten_blocks(query_grads[layer_idx], inv_in, inv_out, proj_rank)
        running = running + score_block(whitened, train_grads)
    return running
```

```python
import functools
import math

import jax
import jax.numpy as jnp
import numpy as np
from jax import lax
from jax.experimental import pallas as pl
from jax.experimental.pallas import tpu as pltpu
from jax.sharding import Mesh, PartitionSpec as P

SEQ = 64
DAMPING = 0.1
HIGH = lax.Precision.HIGHEST
F32 = jnp.float32
BF16 = jnp.bfloat16

PAIR = [(0, 1)]
RING4 = [[(0, 1), (2, 3)], [(1, 2), (3, 0)]]
RING8 = [
    [(0, 1), (2, 3), (4, 5), (6, 7)],
    [(1, 2), (3, 4), (5, 6), (7, 0)],
    [(1, 6), (2, 5), (0, 3), (7, 4)],
]


def swap(value, axis, pairs):
    return lax.ppermute(value, axis, pairs + [(b, a) for a, b in pairs])


def ring8_order():
    held = [[z] for z in range(8)]
    for pairs in RING8:
        partner = {}
        for a, b in pairs:
            partner[a], partner[b] = b, a
        held = [held[z] + held[partner[z]] for z in range(8)]
    return np.array(held, np.int32)


def project_kernel(acts, grads, tab_in, tab_out, fac, outer, p_in, p_out, *, scale):
    step = pl.program_id(0)

    @pl.when(step == 0)
    def _():
        p_in[...] = ((2 * tab_in[...] - 1).astype(F32) * scale).astype(BF16)
        p_out[...] = ((2 * tab_out[...] - 1).astype(F32) * scale).astype(BF16)
        fac[...] = jnp.zeros_like(fac)

    nt = (((1,), (1,)), ((), ()))
    x = lax.dot_general(acts[...], p_in[...], nt, preferred_element_type=F32)
    g = lax.dot_general(grads[...], p_out[...], nt, preferred_element_type=F32)
    both = jnp.concatenate([x, g], axis=1)
    rank = x.shape[1]
    left = lax.broadcasted_iota(jnp.int32, (rank, 2 * rank), 1) < rank
    blocks = []
    total = fac[...]
    for e in range(both.shape[0] // SEQ):
        rows = both[e * SEQ : (e + 1) * SEQ]
        gram = lax.dot_general(
            rows, rows, (((0,), (0,)), ((), ())), precision=HIGH, preferred_element_type=F32
        )
        total = total + jnp.where(left, gram[:rank], gram[rank:])
        blocks.append(gram[rank:, :rank])
    fac[...] = total
    outer[...] = jnp.concatenate(blocks, axis=1).astype(BF16)


def project(acts, grads, tab_in, tab_out):
    tokens, width = acts.shape
    rank = tab_in.shape[0]
    chunk = 128
    wide = chunk // SEQ * rank
    return pl.pallas_call(
        functools.partial(project_kernel, scale=1.0 / math.sqrt(width)),
        grid=(tokens // chunk,),
        in_specs=[
            pl.BlockSpec((chunk, width), lambda i: (i, 0)),
            pl.BlockSpec((chunk, width), lambda i: (i, 0)),
            pl.BlockSpec((rank, width), lambda i: (0, 0)),
            pl.BlockSpec((rank, width), lambda i: (0, 0)),
        ],
        out_specs=[
            pl.BlockSpec((rank, 2 * rank), lambda i: (0, 0)),
            pl.BlockSpec((rank, wide), lambda i: (0, i)),
        ],
        out_shape=[
            jax.ShapeDtypeStruct((rank, 2 * rank), F32),
            jax.ShapeDtypeStruct((rank, tokens // SEQ * rank), BF16),
        ],
        scratch_shapes=[pltpu.VMEM((rank, width), BF16), pltpu.VMEM((rank, width), BF16)],
        compiler_params=pltpu.CompilerParams(
            dimension_semantics=("arbitrary",), vmem_limit_bytes=40 * 2**20
        ),
        cost_estimate=pl.CostEstimate(
            flops=4 * tokens * width * rank, bytes_accessed=10 * 2**20, transcendentals=0
        ),
        name="project",
    )(acts, grads, tab_in, tab_out)


def invert_pair(mat):
    rank = mat.shape[0]
    lane = lax.broadcasted_iota(jnp.int32, (1, 2 * rank), 1)
    row = lax.broadcasted_iota(jnp.int32, (rank, 1), 0)
    left = lane < rank
    for k in range(rank):
        at = (lane & (rank - 1)) == k
        col = jnp.where(left, mat[:, k : k + 1], mat[:, rank + k : rank + k + 1])
        inv = 1.0 / col[k : k + 1]
        scaled = jnp.where(at, 1.0, mat[k : k + 1]) * inv
        mat = jnp.where(row == k, scaled, jnp.where(at, 0.0, mat) - col * scaled)
    return mat


def halves(value):
    hi = value.astype(BF16)
    return hi, (value - hi.astype(F32)).astype(BF16)


def whiten_kernel(fac, outer, out, held, *, tokens):
    rank = fac.shape[0]
    mat = fac[...] / tokens
    lane = lax.broadcasted_iota(jnp.int32, (rank, 2 * rank), 1)
    row = lax.broadcasted_iota(jnp.int32, (rank, 2 * rank), 0)
    left = lane < rank
    diag = jnp.where((lane & (rank - 1)) == row, mat, 0.0)
    ridge_in = DAMPING * jnp.sum(jnp.where(left, diag, 0.0), keepdims=True) / rank
    ridge_out = DAMPING * jnp.sum(jnp.where(left, 0.0, diag), keepdims=True) / rank
    ridge = jnp.where(left, ridge_in, ridge_out)
    mat = invert_pair(mat + jnp.where((lane & (rank - 1)) == row, ridge, 0.0))
    inv_in = mat[:, :rank]
    inv_out = mat[:, rank:]
    out_hi, out_lo = halves(inv_out)
    four = 4 * rank
    rows4 = lax.broadcasted_iota(jnp.int32, (four, four), 0) // rank
    cols4 = lax.broadcasted_iota(jnp.int32, (four, four), 1) // rank
    wide = jnp.concatenate([inv_in] * 4, axis=1)
    wide = jnp.concatenate([wide] * 4, axis=0)
    in_hi, in_lo = halves(jnp.where(rows4 == cols4, wide, 0.0))
    dot = functools.partial(jnp.dot, preferred_element_type=F32)
    places = outer.shape[0] // rank
    for p in range(places):
        part = outer[p * rank : (p + 1) * rank]
        first = dot(out_hi, part) + dot(out_lo, part)
        hi, lo = halves(first)
        for c in range(outer.shape[1] // four):
            cut = slice(c * four, (c + 1) * four)
            held[p, :, cut] = dot(hi[:, cut], in_hi) + (
                dot(hi[:, cut], in_lo) + dot(lo[:, cut], in_hi)
            )
    low = lax.broadcasted_iota(jnp.int32, (places, 2 * rank), 1) < rank
    for o in range(0, rank, 2):
        even = held[:, o, :]
        odd = held[:, o + 1, :]
        pieces = []
        for pair in range(outer.shape[1] // (2 * rank)):
            cut = slice(pair * 2 * rank, (pair + 1) * 2 * rank)
            a, b = even[:, cut], odd[:, cut]
            pieces.append(jnp.where(low, a, pltpu.roll(b, rank, 1)))
            pieces.append(jnp.where(low, pltpu.roll(a, rank, 1), b))
        out[:, o * rank : (o + 2) * rank] = jnp.concatenate(pieces, axis=0).astype(BF16)


def whiten(fac, outer, tokens):
    rank = fac.shape[0]
    places = outer.shape[0] // rank
    examples = outer.shape[1] // rank
    return pl.pallas_call(
        functools.partial(whiten_kernel, tokens=tokens),
        out_shape=jax.ShapeDtypeStruct((places * examples, rank * rank), BF16),
        scratch_shapes=[pltpu.VMEM((places, rank, outer.shape[1]), F32)],
        compiler_params=pltpu.CompilerParams(vmem_limit_bytes=40 * 2**20),
        cost_estimate=pl.CostEstimate(
            flops=12 * 512 * 512 * 256, bytes_accessed=2**20, transcendentals=0
        ),
        name="whiten",
    )(fac, outer)


def score_kernel(order, train, queries, out, held):
    both = lax.dot_general(
        train[...], queries[...], (((1,), (1,)), ((), ())), preferred_element_type=F32
    )
    for b in range(held.shape[0]):
        held[b] = both[:, b * 128 : (b + 1) * 128]
    places = order.shape[0]
    groups = out.shape[0] // places
    wide = both.shape[1] // groups
    half = out.shape[1]
    for p in range(places):
        for g in range(groups):
            block, at = divmod(g * wide, 128)
            rows = held[block, pl.ds(p, held.shape[1] // places, places), :]
            cut = rows[:, at : at + wide]
            out[order[p] * groups + g] = jnp.concatenate([cut[:half], cut[half:]], axis=1)


def score(order, train, queries, groups):
    places = order.shape[0]
    per_place = train.shape[0] // places
    return pl.pallas_call(
        score_kernel,
        out_shape=jax.ShapeDtypeStruct(
            (places * groups, per_place // 2, 2 * queries.shape[0] // groups), F32
        ),
        in_specs=[
            pl.BlockSpec(memory_space=pltpu.SMEM),
            pl.BlockSpec(memory_space=pltpu.VMEM),
            pl.BlockSpec(memory_space=pltpu.VMEM),
        ],
        scratch_shapes=[pltpu.VMEM((queries.shape[0] // 128, train.shape[0], 128), F32)],
        compiler_params=pltpu.CompilerParams(vmem_limit_bytes=40 * 2**20),
        cost_estimate=pl.CostEstimate(
            flops=2 * train.shape[0] * train.shape[1] * queries.shape[0],
            bytes_accessed=3 * 2**20,
            transcendentals=0,
        ),
        name="score",
    )(order, train, queries)


def collect_kernel(parts, out, *, groups):
    places = parts.shape[0] // groups
    half, wide = parts.shape[1], parts.shape[2] // 2
    runs = wide // 2
    tops, bottoms = [], []
    for p in range(places):
        total = parts[p * groups]
        for g in range(1, groups):
            total = total + parts[p * groups + g]
        tops.append(total[:, :wide])
        bottoms.append(total[:, wide:])
    for rows, cuts in ((0, tops), (half, bottoms)):
        line = [cut[:, r * runs : (r + 1) * runs] for r in range(2) for cut in cuts]
        out[rows : rows + half, :] = jnp.concatenate(line, axis=1)


def collect(parts, groups):
    places = parts.shape[0] // groups
    return pl.pallas_call(
        functools.partial(collect_kernel, groups=groups),
        out_shape=jax.ShapeDtypeStruct(
            (2 * parts.shape[1], places * parts.shape[2] // 2), F32
        ),
        name="collect",
    )(parts)


def per_device(acts, out_grads, proj_in, proj_out, query_grads):
    groups = lax.axis_size("yh") * lax.axis_size("core")
    queries = lax.all_gather(query_grads[0], ("yl", "x"), axis=0, tiled=True)
    order = jnp.asarray(ring8_order())[lax.axis_index("z")]
    fac, outer = project(acts[0], out_grads[0], proj_in[0], proj_out[0])
    for pairs in RING8:
        fac = fac + swap(fac, "z", pairs)
        outer = jnp.concatenate([outer, swap(outer, "z", pairs)], axis=0)
    for pairs in RING4:
        fac = fac + swap(fac, "x", pairs)
    fac = fac + swap(fac, "yl", PAIR)
    tokens = acts.shape[1] * lax.axis_size(("yl", "x", "z"))
    train = whiten(fac, outer, tokens)
    parts = score(order, train, queries, groups)
    parts = lax.all_to_all(parts, ("z", "yh", "core"), 0, 0, tiled=True)
    return collect(parts, groups).T


def solution(mesh):
    split = Mesh(mesh.devices.reshape(2, 4, 8, 2, 2), ("yl", "x", "z", "yh", "core"))
    dp, grp = ("yl", "x", "z"), ("yh", "core")
    return jax.shard_map(
        per_device,
        mesh=split,
        in_specs=(
            P(grp, dp, None),
            P(grp, dp, None),
            P(grp, None, None),
            P(grp, None, None),
            P(grp, dp, None),
        ),
        out_specs=P(grp, dp),
        check_vma=False,
    )
```

```python
import functools
import math

import jax
import jax.numpy as jnp
import numpy as np
from jax import lax
from jax.experimental import pallas as pl
from jax.experimental.pallas import tpu as pltpu
from jax.sharding import Mesh, PartitionSpec as P

SEQ = 64
DAMPING = 0.1
HIGH = lax.Precision.HIGHEST
F32 = jnp.float32
BF16 = jnp.bfloat16

PAIR = [(0, 1)]
RING4 = [[(0, 1), (2, 3)], [(1, 2), (3, 0)]]
RING8 = [
    [(0, 1), (2, 3), (4, 5), (6, 7)],
    [(1, 2), (3, 4), (5, 6), (7, 0)],
    [(1, 6), (2, 5), (0, 3), (7, 4)],
]


def swap(value, axis, pairs):
    return lax.ppermute(value, axis, pairs + [(b, a) for a, b in pairs])


def gathered(rings, size):
    held = [[z] for z in range(size)]
    for pairs in rings:
        partner = {}
        for a, b in pairs:
            partner[a], partner[b] = b, a
        held = [held[z] + held[partner[z]] for z in range(size)]
    return held


def layouts():
    trains, pairs = gathered(RING8, 8), gathered(RING4, 4)
    table = np.zeros((2, 4, 8, 16), np.int32)
    for y, x, z in np.ndindex(2, 4, 8):
        at = pairs[x]
        groups = [(y ^ i) * 2 + at[2 * j] // 2 for i in range(2) for j in range(2)]
        table[y, x, z, :14] = trains[z] + groups + [at[0] % 2, at[2] % 2]
    return table


def project_kernel(acts, grads, tab_in, tab_out, fac, outer, p_in, p_out, *, scale):
    step = pl.program_id(0)

    @pl.when(step == 0)
    def _():
        p_in[...] = ((2 * tab_in[...] - 1).astype(F32) * scale).astype(BF16)
        p_out[...] = ((2 * tab_out[...] - 1).astype(F32) * scale).astype(BF16)
        fac[...] = jnp.zeros_like(fac)

    nt = (((1,), (1,)), ((), ()))
    x = lax.dot_general(acts[...], p_in[...], nt, preferred_element_type=F32)
    g = lax.dot_general(grads[...], p_out[...], nt, preferred_element_type=F32)
    both = jnp.concatenate([x, g], axis=1)
    rank = x.shape[1]
    left = lax.broadcasted_iota(jnp.int32, (rank, 2 * rank), 1) < rank
    blocks = []
    total = fac[...]
    for e in range(both.shape[0] // SEQ):
        rows = both[e * SEQ : (e + 1) * SEQ]
        gram = lax.dot_general(
            rows, rows, (((0,), (0,)), ((), ())), precision=HIGH, preferred_element_type=F32
        )
        total = total + jnp.where(left, gram[:rank], gram[rank:])
        blocks.append(gram[rank:, :rank])
    fac[...] = total
    outer[...] = jnp.concatenate(blocks, axis=1).astype(BF16)


def project(acts, grads, tab_in, tab_out):
    tokens, width = acts.shape
    rank = tab_in.shape[0]
    chunk = 256
    wide = chunk // SEQ * rank
    return pl.pallas_call(
        functools.partial(project_kernel, scale=1.0 / math.sqrt(width)),
        grid=(tokens // chunk,),
        in_specs=[
            pl.BlockSpec((chunk, width), lambda i: (i, 0)),
            pl.BlockSpec((chunk, width), lambda i: (i, 0)),
            pl.BlockSpec((rank, width), lambda i: (0, 0), pipeline_mode=pl.Buffered(1)),
            pl.BlockSpec((rank, width), lambda i: (0, 0), pipeline_mode=pl.Buffered(1)),
        ],
        out_specs=[
            pl.BlockSpec((rank, 2 * rank), lambda i: (0, 0)),
            pl.BlockSpec((rank, wide), lambda i: (0, i)),
        ],
        out_shape=[
            jax.ShapeDtypeStruct((rank, 2 * rank), F32),
            jax.ShapeDtypeStruct((rank, tokens // SEQ * rank), BF16),
        ],
        scratch_shapes=[pltpu.VMEM((rank, width), BF16), pltpu.VMEM((rank, width), BF16)],
        compiler_params=pltpu.CompilerParams(
            dimension_semantics=("arbitrary",), vmem_limit_bytes=60 * 2**20
        ),
        cost_estimate=pl.CostEstimate(
            flops=4 * tokens * width * rank, bytes_accessed=10 * 2**20, transcendentals=0
        ),
        name="project",
    )(acts, grads, tab_in, tab_out)


def solve_two(a, b, c, d, top, bottom):
    inv = 1.0 / (a * d - b * c)
    return (d * top - b * bottom) * inv, (a * bottom - c * top) * inv


def invert_pair(mat):
    rank = mat.shape[0]
    lane = lax.broadcasted_iota(jnp.int32, (1, 2 * rank), 1)
    row = lax.broadcasted_iota(jnp.int32, (rank, 1), 0)
    left = lane < rank
    place = lane & (rank - 1)
    for k in range(0, rank, 4):
        cols = [
            jnp.where(left, mat[:, k + i : k + i + 1], mat[:, rank + k + i : rank + k + i + 1])
            for i in range(4)
        ]
        m = [[cols[j][k + i : k + i + 1] for j in range(4)] for i in range(4)]
        rows = []
        for i in range(4):
            line = mat[k + i : k + i + 1]
            for j in range(4):
                line = jnp.where(place == k + j, 1.0 if i == j else 0.0, line)
            rows.append(line)
        head = m[0][0], m[0][1], m[1][0], m[1][1]
        u0, u1 = solve_two(*head, rows[0], rows[1])
        p0, p1 = solve_two(*head, m[0][2], m[1][2])
        q0, q1 = solve_two(*head, m[0][3], m[1][3])
        schur = (
            m[2][2] - m[2][0] * p0 - m[2][1] * p1,
            m[2][3] - m[2][0] * q0 - m[2][1] * q1,
            m[3][2] - m[3][0] * p0 - m[3][1] * p1,
            m[3][3] - m[3][0] * q0 - m[3][1] * q1,
        )
        t0 = rows[2] - m[2][0] * u0 - m[2][1] * u1
        t1 = rows[3] - m[3][0] * u0 - m[3][1] * u1
        v0, v1 = solve_two(*schur, t0, t1)
        solved = [u0 - p0 * v0 - q0 * v1, u1 - p1 * v0 - q1 * v1, v0, v1]
        rest = jnp.where((place >= k) & (place < k + 4), 0.0, mat)
        for i in range(4):
            rest = rest - cols[i] * solved[i]
        for i in range(4):
            rest = jnp.where(row == k + i, solved[i], rest)
        mat = rest
    return mat


def halves(value):
    hi = value.astype(BF16)
    return hi, (value - hi.astype(F32)).astype(BF16)


def whiten_kernel(fac, outer, out, held, *, tokens):
    rank = fac.shape[0]
    mat = fac[...] / tokens
    lane = lax.broadcasted_iota(jnp.int32, (rank, 2 * rank), 1)
    row = lax.broadcasted_iota(jnp.int32, (rank, 2 * rank), 0)
    left = lane < rank
    diag = jnp.where((lane & (rank - 1)) == row, mat, 0.0)
    ridge_in = DAMPING * jnp.sum(jnp.where(left, diag, 0.0), keepdims=True) / rank
    ridge_out = DAMPING * jnp.sum(jnp.where(left, 0.0, diag), keepdims=True) / rank
    ridge = jnp.where(left, ridge_in, ridge_out)
    mat = invert_pair(mat + jnp.where((lane & (rank - 1)) == row, ridge, 0.0))
    inv_in = mat[:, :rank]
    inv_out = mat[:, rank:]
    out_hi, out_lo = halves(inv_out)
    four = 4 * rank
    rows4 = lax.broadcasted_iota(jnp.int32, (four, four), 0) // rank
    cols4 = lax.broadcasted_iota(jnp.int32, (four, four), 1) // rank
    wide = jnp.concatenate([inv_in] * 4, axis=1)
    wide = jnp.concatenate([wide] * 4, axis=0)
    in_hi, in_lo = halves(jnp.where(rows4 == cols4, wide, 0.0))
    dot = functools.partial(jnp.dot, preferred_element_type=F32)
    places = outer.shape[0] // rank
    for p in range(places):
        part = outer[p * rank : (p + 1) * rank]
        first = dot(out_hi, part) + dot(out_lo, part)
        hi, lo = halves(first)
        for c in range(outer.shape[1] // four):
            cut = slice(c * four, (c + 1) * four)
            held[p, :, cut] = dot(hi[:, cut], in_hi) + (
                dot(hi[:, cut], in_lo) + dot(lo[:, cut], in_hi)
            )
    low = lax.broadcasted_iota(jnp.int32, (places, 2 * rank), 1) < rank
    for o in range(0, rank, 2):
        even = held[:, o, :]
        odd = held[:, o + 1, :]
        pieces = []
        for pair in range(outer.shape[1] // (2 * rank)):
            cut = slice(pair * 2 * rank, (pair + 1) * 2 * rank)
            a, b = even[:, cut], odd[:, cut]
            pieces.append(jnp.where(low, a, pltpu.roll(b, rank, 1)))
            pieces.append(jnp.where(low, pltpu.roll(a, rank, 1), b))
        out[:, o * rank : (o + 2) * rank] = jnp.concatenate(pieces, axis=0).astype(BF16)


def whiten(fac, outer, tokens):
    rank = fac.shape[0]
    places = outer.shape[0] // rank
    examples = outer.shape[1] // rank
    return pl.pallas_call(
        functools.partial(whiten_kernel, tokens=tokens),
        out_shape=jax.ShapeDtypeStruct((places * examples, rank * rank), BF16),
        scratch_shapes=[pltpu.VMEM((places, rank, outer.shape[1]), F32)],
        compiler_params=pltpu.CompilerParams(vmem_limit_bytes=16 * 2**20),
        cost_estimate=pl.CostEstimate(
            flops=12 * 512 * 512 * 256, bytes_accessed=2**20, transcendentals=0
        ),
        name="whiten",
    )(fac, outer)


def score_kernel(layout, train, near, far, out, held, *, places):
    nt = (((1,), (1,)), ((), ()))
    for i, queries in enumerate((near, far)):
        held[i] = lax.dot_general(train[...], queries[...], nt, preferred_element_type=F32)
    examples = held.shape[1] // places
    half = examples // 2
    run = held.shape[2] // 4
    for p in range(places):
        for i in range(2):
            rows = held[i, pl.ds(p, examples, places), :]
            for j in range(2):
                pair = rows[:, 2 * j * run : 2 * (j + 1) * run]
                turned = jnp.concatenate([pair[:, run:], pair[:, :run]], axis=1)
                cut = jnp.where(layout[places + 4 + j] == 1, turned, pair)
                target = layout[p] * 4 + layout[places + 2 * i + j]
                out[target] = jnp.concatenate([cut[:half], cut[half:]], axis=1)


def score(layout, train, near, far, places):
    examples = train.shape[0] // places
    return pl.pallas_call(
        functools.partial(score_kernel, places=places),
        out_shape=jax.ShapeDtypeStruct((places * 4, examples // 2, near.shape[0]), F32),
        in_specs=[pl.BlockSpec(memory_space=pltpu.SMEM)]
        + [pl.BlockSpec(memory_space=pltpu.VMEM)] * 3,
        scratch_shapes=[pltpu.VMEM((2, train.shape[0], near.shape[0]), F32)],
        compiler_params=pltpu.CompilerParams(vmem_limit_bytes=16 * 2**20),
        cost_estimate=pl.CostEstimate(
            flops=4 * train.shape[0] * train.shape[1] * near.shape[0],
            bytes_accessed=3 * 2**20,
            transcendentals=0,
        ),
        name="score",
    )(layout, train, near, far)


def collect_kernel(parts, out, *, groups):
    places = parts.shape[0] // groups
    half, wide = parts.shape[1], parts.shape[2] // 2
    runs = wide // 2
    tops, bottoms = [], []
    for p in range(places):
        total = parts[p * groups]
        for g in range(1, groups):
            total = total + parts[p * groups + g]
        tops.append(total[:, :wide])
        bottoms.append(total[:, wide:])
    for rows, cuts in ((0, tops), (half, bottoms)):
        line = [cut[:, r * runs : (r + 1) * runs] for r in range(2) for cut in cuts]
        out[rows : rows + half, :] = jnp.concatenate(line, axis=1)


def collect(parts, groups):
    places = parts.shape[0] // groups
    return pl.pallas_call(
        functools.partial(collect_kernel, groups=groups),
        out_shape=jax.ShapeDtypeStruct(
            (2 * parts.shape[1], places * parts.shape[2] // 2), F32
        ),
        name="collect",
    )(parts)


def per_device(acts, out_grads, proj_in, proj_out, query_grads):
    places, groups = lax.axis_size("z"), lax.axis_size(("yh", "core"))
    near = query_grads[0]
    near = jnp.concatenate([near, swap(near, "x", RING4[0])], axis=0)
    layout = jnp.asarray(layouts())[
        lax.axis_index("yl"), lax.axis_index("x"), lax.axis_index("z")
    ]
    fac, outer = project(acts[0], out_grads[0], proj_in[0], proj_out[0])
    fac, near = lax.optimization_barrier((fac, near))
    fac = fac + swap(fac, "yl", PAIR)
    outer = jnp.concatenate([outer, swap(outer, "z", RING8[0])], axis=0)
    fac, near = lax.optimization_barrier((fac, near))
    fac = fac + swap(fac, "z", RING8[0])
    near = jnp.concatenate([near, swap(near, "x", RING4[1])], axis=0)
    fac, outer = lax.optimization_barrier((fac, outer))
    fac = fac + swap(fac, "z", RING8[1])
    outer = jnp.concatenate([outer, swap(outer, "z", RING8[1])], axis=0)
    fac, near = lax.optimization_barrier((fac, near))
    fac = fac + swap(fac, "z", RING8[2])
    far = swap(near, "yl", PAIR)
    fac, outer = lax.optimization_barrier((fac, outer))
    fac = fac + swap(fac, "x", RING4[0])
    outer = jnp.concatenate([outer, swap(outer, "z", RING8[2])], axis=0)
    fac = fac + swap(fac, "x", RING4[1])
    tokens = acts.shape[1] * lax.axis_size(("yl", "x", "z"))
    train = whiten(fac, outer, tokens)
    parts = score(layout, train, near, far, places)
    parts = lax.all_to_all(parts, ("z", "yh", "core"), 0, 0, tiled=True)
    return collect(parts, groups).T


def solution(mesh):
    split = Mesh(mesh.devices.reshape(2, 4, 8, 2, 2), ("yl", "x", "z", "yh", "core"))
    dp, grp = ("yl", "x", "z"), ("yh", "core")
    return jax.shard_map(
        per_device,
        mesh=split,
        in_specs=(
            P(grp, dp, None),
            P(grp, dp, None),
            P(grp, None, None),
            P(grp, None, None),
            P(grp, dp, None),
        ),
        out_specs=P(grp, dp),
        check_vma=False,
    )
```

```python
import functools
import math

import jax
import jax.numpy as jnp
import numpy as np
from jax import lax
from jax.experimental import pallas as pl
from jax.experimental.pallas import tpu as pltpu
from jax.sharding import Mesh, PartitionSpec as P

SEQ = 64
DAMPING = 0.1
HIGH = lax.Precision.HIGHEST
F32 = jnp.float32
BF16 = jnp.bfloat16

PAIR = [(0, 1)]
RING4 = [[(0, 1), (2, 3)], [(1, 2), (3, 0)]]
RING8 = [
    [(0, 1), (2, 3), (4, 5), (6, 7)],
    [(1, 2), (3, 4), (5, 6), (7, 0)],
    [(1, 6), (2, 5), (0, 3), (7, 4)],
]


def swap(value, axis, pairs):
    return lax.ppermute(value, axis, pairs + [(b, a) for a, b in pairs])


def gathered(rings, size):
    held = [[z] for z in range(size)]
    for pairs in rings:
        partner = {}
        for a, b in pairs:
            partner[a], partner[b] = b, a
        held = [held[z] + held[partner[z]] for z in range(size)]
    return held


def layouts():
    trains, pairs = gathered(RING8, 8), gathered(RING4, 4)
    table = np.zeros((2, 4, 8, 16), np.int32)
    for y, x, z in np.ndindex(2, 4, 8):
        at = pairs[x]
        groups = [(y ^ i) * 2 + at[2 * j] // 2 for i in range(2) for j in range(2)]
        table[y, x, z, :14] = trains[z] + groups + [at[0] % 2, at[2] % 2]
    return table


def project_kernel(
    acts, grads, tab_in, tab_out, fac, outer, acts_v, grads_v, in_v, out_v, sems, *, scale, chunk
):
    tokens, width = acts.shape
    rank = tab_in.shape[0]
    cuts = [(slice(None), pl.ds(at, chunk)) for at in range(0, width, chunk)]
    arrays = ((tab_in, in_v), (tab_out, out_v), (acts, acts_v), (grads, grads_v))
    loads = [
        [
            pltpu.make_async_copy(source.at[cut], target.at[cut], sems.at[4 * i + j])
            for j, (source, target) in enumerate(arrays)
        ]
        for i, cut in enumerate(cuts)
    ]
    for load in loads:
        for copy in load:
            copy.start()

    def part(values, table, cut):
        matrix = ((2 * table[cut] - 1).astype(F32) * scale).astype(BF16)
        return lax.dot_general(
            values[cut], matrix, (((1,), (1,)), ((), ())), preferred_element_type=F32
        )

    x = g = jnp.zeros((tokens, rank), F32)
    for load, cut in zip(loads, cuts):
        for copy in load:
            copy.wait()
        x = x + part(acts_v, in_v, cut)
        g = g + part(grads_v, out_v, cut)
    both = jnp.concatenate([x, g], axis=1)
    left = lax.broadcasted_iota(jnp.int32, (rank, 2 * rank), 1) < rank
    total = jnp.zeros((rank, 2 * rank), F32)
    blocks = []
    for e in range(tokens // SEQ):
        rows = both[e * SEQ : (e + 1) * SEQ]
        gram = lax.dot_general(
            rows, rows, (((0,), (0,)), ((), ())), precision=HIGH, preferred_element_type=F32
        )
        total = total + jnp.where(left, gram[:rank], gram[rank:])
        blocks.append(gram[rank:, :rank])
    fac[...] = total
    outer[...] = jnp.concatenate(blocks, axis=1).astype(BF16)


def project(acts, grads, tab_in, tab_out):
    tokens, width = acts.shape
    rank = tab_in.shape[0]
    chunk = 256
    return pl.pallas_call(
        functools.partial(project_kernel, scale=1.0 / math.sqrt(width), chunk=chunk),
        in_specs=[pl.BlockSpec(memory_space=pl.ANY)] * 4,
        out_specs=[pl.BlockSpec(memory_space=pltpu.VMEM)] * 2,
        out_shape=[
            jax.ShapeDtypeStruct((rank, 2 * rank), F32),
            jax.ShapeDtypeStruct((rank, tokens // SEQ * rank), BF16),
        ],
        scratch_shapes=[
            pltpu.VMEM((tokens, width), BF16),
            pltpu.VMEM((tokens, width), BF16),
            pltpu.VMEM((rank, width), jnp.int32),
            pltpu.VMEM((rank, width), jnp.int32),
            pltpu.SemaphoreType.DMA((4 * width // chunk,)),
        ],
        compiler_params=pltpu.CompilerParams(vmem_limit_bytes=53 * 2**20 + 2**18),
        cost_estimate=pl.CostEstimate(
            flops=4 * tokens * width * rank, bytes_accessed=10 * 2**20, transcendentals=0
        ),
        name="project",
    )(acts, grads, tab_in, tab_out)


def solve_two(a, b, c, d, top, bottom):
    inv = 1.0 / (a * d - b * c)
    return (d * top - b * bottom) * inv, (a * bottom - c * top) * inv


def invert_pair(mat):
    rank = mat.shape[0]
    lane = lax.broadcasted_iota(jnp.int32, (1, 2 * rank), 1)
    row = lax.broadcasted_iota(jnp.int32, (rank, 1), 0)
    left = lane < rank
    place = lane & (rank - 1)
    for k in range(0, rank, 4):
        cols = [
            jnp.where(left, mat[:, k + i : k + i + 1], mat[:, rank + k + i : rank + k + i + 1])
            for i in range(4)
        ]
        m = [[cols[j][k + i : k + i + 1] for j in range(4)] for i in range(4)]
        rows = []
        for i in range(4):
            line = mat[k + i : k + i + 1]
            for j in range(4):
                line = jnp.where(place == k + j, 1.0 if i == j else 0.0, line)
            rows.append(line)
        head = m[0][0], m[0][1], m[1][0], m[1][1]
        u0, u1 = solve_two(*head, rows[0], rows[1])
        p0, p1 = solve_two(*head, m[0][2], m[1][2])
        q0, q1 = solve_two(*head, m[0][3], m[1][3])
        schur = (
            m[2][2] - m[2][0] * p0 - m[2][1] * p1,
            m[2][3] - m[2][0] * q0 - m[2][1] * q1,
            m[3][2] - m[3][0] * p0 - m[3][1] * p1,
            m[3][3] - m[3][0] * q0 - m[3][1] * q1,
        )
        t0 = rows[2] - m[2][0] * u0 - m[2][1] * u1
        t1 = rows[3] - m[3][0] * u0 - m[3][1] * u1
        v0, v1 = solve_two(*schur, t0, t1)
        solved = [u0 - p0 * v0 - q0 * v1, u1 - p1 * v0 - q1 * v1, v0, v1]
        rest = jnp.where((place >= k) & (place < k + 4), 0.0, mat)
        for i in range(4):
            rest = rest - cols[i] * solved[i]
        for i in range(4):
            rest = jnp.where(row == k + i, solved[i], rest)
        mat = rest
    return mat


def halves(value):
    hi = value.astype(BF16)
    return hi, (value - hi.astype(F32)).astype(BF16)


def invert_kernel(fac, out, *, tokens):
    rank = fac.shape[0]
    mat = fac[...] / tokens
    lane = lax.broadcasted_iota(jnp.int32, (rank, 2 * rank), 1)
    row = lax.broadcasted_iota(jnp.int32, (rank, 2 * rank), 0)
    left = lane < rank
    diag = jnp.where((lane & (rank - 1)) == row, mat, 0.0)
    ridge_in = DAMPING * jnp.sum(jnp.where(left, diag, 0.0), keepdims=True) / rank
    ridge_out = DAMPING * jnp.sum(jnp.where(left, 0.0, diag), keepdims=True) / rank
    ridge = jnp.where(left, ridge_in, ridge_out)
    out[...] = invert_pair(mat + jnp.where((lane & (rank - 1)) == row, ridge, 0.0))


def invert(fac, tokens):
    return pl.pallas_call(
        functools.partial(invert_kernel, tokens=tokens),
        out_shape=jax.ShapeDtypeStruct(fac.shape, F32),
        compiler_params=pltpu.CompilerParams(vmem_limit_bytes=4 * 2**20),
        cost_estimate=pl.CostEstimate(
            flops=25 * 10**8, bytes_accessed=2**16, transcendentals=0
        ),
        name="invert",
    )(fac)


def whiten_kernel(inverses, near, far, out, held):
    rank = inverses.shape[0]
    mat = inverses[...]
    inv_in = mat[:, :rank]
    inv_out = mat[:, rank:]
    out_hi, out_lo = halves(inv_out)
    four = 4 * rank
    rows4 = lax.broadcasted_iota(jnp.int32, (four, four), 0) // rank
    cols4 = lax.broadcasted_iota(jnp.int32, (four, four), 1) // rank
    tiled = jnp.concatenate([inv_in] * 4, axis=1)
    tiled = jnp.concatenate([tiled] * 4, axis=0)
    in_hi, in_lo = halves(jnp.where(rows4 == cols4, tiled, 0.0))
    dot = functools.partial(jnp.dot, preferred_element_type=F32)
    half = near.shape[0] // rank
    places = 2 * half
    wide = near.shape[1]
    for p in range(places):
        at = p % half * rank
        part = (near if p < half else far)[at : at + rank, :]
        first = dot(out_hi, part) + dot(out_lo, part)
        hi, lo = halves(first)
        for c in range(wide // four):
            cut = slice(c * four, (c + 1) * four)
            held[p, :, cut] = dot(hi[:, cut], in_hi) + (
                dot(hi[:, cut], in_lo) + dot(lo[:, cut], in_hi)
            )
    low = lax.broadcasted_iota(jnp.int32, (places, 2 * rank), 1) < rank
    for o in range(0, rank, 2):
        even = held[:, o, :]
        odd = held[:, o + 1, :]
        pieces = []
        for pair in range(wide // (2 * rank)):
            cut = slice(pair * 2 * rank, (pair + 1) * 2 * rank)
            a, b = even[:, cut], odd[:, cut]
            pieces.append(jnp.where(low, a, pltpu.roll(b, rank, 1)))
            pieces.append(jnp.where(low, pltpu.roll(a, rank, 1), b))
        out[:, o * rank : (o + 2) * rank] = jnp.concatenate(pieces, axis=0).astype(BF16)


def whiten(inverses, near, far):
    rank = inverses.shape[0]
    places = 2 * near.shape[0] // rank
    examples = near.shape[1] // rank
    return pl.pallas_call(
        whiten_kernel,
        out_shape=jax.ShapeDtypeStruct((places * examples, rank * rank), BF16),
        scratch_shapes=[pltpu.VMEM((places, rank, near.shape[1]), F32)],
        compiler_params=pltpu.CompilerParams(vmem_limit_bytes=16 * 2**20),
        cost_estimate=pl.CostEstimate(
            flops=60 * 10**8, bytes_accessed=2**20, transcendentals=0
        ),
        name="whiten",
    )(inverses, near, far)


def score_kernel(layout, train, near, far, out, held, *, places):
    nt = (((1,), (1,)), ((), ()))
    for i, queries in enumerate((near, far)):
        held[i] = lax.dot_general(train[...], queries[...], nt, preferred_element_type=F32)
    examples = held.shape[1] // places
    half = examples // 2
    run = held.shape[2] // 4
    for p in range(places):
        for i in range(2):
            rows = held[i, pl.ds(p, examples, places), :]
            for j in range(2):
                pair = rows[:, 2 * j * run : 2 * (j + 1) * run]
                turned = jnp.concatenate([pair[:, run:], pair[:, :run]], axis=1)
                cut = jnp.where(layout[places + 4 + j] == 1, turned, pair)
                target = layout[p] * 4 + layout[places + 2 * i + j]
                out[target] = jnp.concatenate([cut[:half], cut[half:]], axis=1)


def score(layout, train, near, far, places):
    examples = train.shape[0] // places
    return pl.pallas_call(
        functools.partial(score_kernel, places=places),
        out_shape=jax.ShapeDtypeStruct((places * 4, examples // 2, near.shape[0]), F32),
        in_specs=[pl.BlockSpec(memory_space=pltpu.SMEM)]
        + [pl.BlockSpec(memory_space=pltpu.VMEM)] * 3,
        scratch_shapes=[pltpu.VMEM((2, train.shape[0], near.shape[0]), F32)],
        compiler_params=pltpu.CompilerParams(vmem_limit_bytes=16 * 2**20),
        cost_estimate=pl.CostEstimate(
            flops=4 * train.shape[0] * train.shape[1] * near.shape[0],
            bytes_accessed=3 * 2**20,
            transcendentals=0,
        ),
        name="score",
    )(layout, train, near, far)


def collect_kernel(parts, out, *, groups):
    places = parts.shape[0] // groups
    half, wide = parts.shape[1], parts.shape[2] // 2
    runs = wide // 2
    tops, bottoms = [], []
    for p in range(places):
        total = parts[p * groups]
        for g in range(1, groups):
            total = total + parts[p * groups + g]
        tops.append(total[:, :wide])
        bottoms.append(total[:, wide:])
    for rows, cuts in ((0, tops), (half, bottoms)):
        line = [cut[:, r * runs : (r + 1) * runs] for r in range(2) for cut in cuts]
        out[rows : rows + half, :] = jnp.concatenate(line, axis=1)


def collect(parts, groups):
    places = parts.shape[0] // groups
    return pl.pallas_call(
        functools.partial(collect_kernel, groups=groups),
        out_shape=jax.ShapeDtypeStruct(
            (2 * parts.shape[1], places * parts.shape[2] // 2), F32
        ),
        compiler_params=pltpu.CompilerParams(vmem_limit_bytes=4 * 2**20),
        name="collect",
    )(parts)


def per_device(acts, out_grads, proj_in, proj_out, query_grads):
    places, groups = lax.axis_size("z"), lax.axis_size(("yh", "core"))
    tie = lax.optimization_barrier
    own = query_grads[0]
    got = swap(own, "x", RING4[0])
    layout = jnp.asarray(layouts())[
        lax.axis_index("yl"), lax.axis_index("x"), lax.axis_index("z")
    ]
    fac, outer = project(acts[0], out_grads[0], proj_in[0], proj_out[0])
    fac, outer, own, got = tie((fac, outer, own, got))
    seen = swap(outer, "z", RING8[0])
    fac = fac + swap(fac, "yl", PAIR)
    own = jnp.concatenate([own, got], axis=0)
    got = swap(own, "x", RING4[1])
    fac = fac + swap(fac, "z", RING8[0])
    fac, outer, seen = tie((fac, outer, seen))
    outer = jnp.concatenate([outer, seen], axis=0)
    seen = swap(outer, "z", RING8[1])
    fac = fac + swap(fac, "z", RING8[1])
    fac, own, got = tie((fac, own, got))
    near = jnp.concatenate([own, got], axis=0)
    far = swap(near, "yl", PAIR)
    fac = fac + swap(fac, "z", RING8[2])
    fac, outer, seen = tie((fac, outer, seen))
    outer = jnp.concatenate([outer, seen], axis=0)
    seen = swap(outer, "z", RING8[2])
    fac = fac + swap(fac, "x", RING4[0])
    fac = fac + swap(fac, "x", RING4[1])
    tokens = acts.shape[1] * lax.axis_size(("yl", "x", "z"))
    inverses = invert(fac, tokens)
    inverses, outer, seen = tie((inverses, outer, seen))
    train = whiten(inverses, outer, seen)
    parts = score(layout, train, near, far, places)
    parts = lax.all_to_all(parts, ("z", "yh", "core"), 0, 0, tiled=True)
    return collect(parts, groups).T


def solution(mesh):
    split = Mesh(mesh.devices.reshape(2, 4, 8, 2, 2), ("yl", "x", "z", "yh", "core"))
    dp, grp = ("yl", "x", "z"), ("yh", "core")
    return jax.shard_map(
        per_device,
        mesh=split,
        in_specs=(
            P(grp, dp, None),
            P(grp, dp, None),
            P(grp, None, None),
            P(grp, None, None),
            P(grp, dp, None),
        ),
        out_specs=P(grp, dp),
        check_vma=False,
    )
```

```python
import functools
import math

import jax
import jax.numpy as jnp
import numpy as np
from jax import lax
from jax.experimental import pallas as pl
from jax.experimental.pallas import tpu as pltpu
from jax.sharding import Mesh, PartitionSpec as P

SEQ = 64
DAMPING = 0.1
HIGH = lax.Precision.HIGHEST
F32 = jnp.float32
BF16 = jnp.bfloat16

PAIR = [(0, 1)]
RING4 = [[(0, 1), (2, 3)], [(1, 2), (3, 0)]]
RING8 = [
    [(0, 5), (1, 4), (2, 7), (3, 6)],
    [(0, 1), (2, 3), (4, 5), (6, 7)],
    [(1, 2), (3, 4), (5, 6), (7, 0)],
]

RING8_LAST = [RING8[1], RING8[2], [(1, 6), (2, 5), (0, 3), (7, 4)]]


def swap(value, axis, pairs):
    return lax.ppermute(value, axis, pairs + [(b, a) for a, b in pairs])


def gathered(rings, size):
    held = [[z] for z in range(size)]
    for pairs in rings:
        partner = {}
        for a, b in pairs:
            partner[a], partner[b] = b, a
        held = [held[z] + held[partner[z]] for z in range(size)]
    return held


def join_kernel(a, b, out):
    rows = a.shape[0]
    out[:rows, :] = a[...]
    out[rows:, :] = b[...]


def join(a, b, work):
    return pl.pallas_call(
        join_kernel,
        out_shape=jax.ShapeDtypeStruct((2 * a.shape[0], a.shape[1]), a.dtype),
        compiler_params=pltpu.CompilerParams(vmem_limit_bytes=4 * 2**20),
        cost_estimate=pl.CostEstimate(flops=work, bytes_accessed=2**20, transcendentals=0),
        name="join",
    )(a, b)


def layouts():
    trains, pairs = gathered(RING8, 8), gathered(RING4, 4)
    table = np.zeros((2, 4, 8, 16), np.int32)
    for y, x, z in np.ndindex(2, 4, 8):
        at = pairs[x]
        groups = [(y ^ i) * 2 + at[2 * j] // 2 for i in range(2) for j in range(2)]
        table[y, x, z, :14] = trains[z] + groups + [at[0] % 2, at[2] % 2]
    return table


def project_kernel(
    acts, grads, tab_in, tab_out, fac, outer, acts_v, grads_v, in_v, out_v, sems, *, scale, chunk
):
    tokens, width = acts.shape
    rank = tab_in.shape[0]
    cuts = [(slice(None), pl.ds(at, chunk)) for at in range(0, width, chunk)]
    arrays = ((tab_in, in_v), (tab_out, out_v), (acts, acts_v), (grads, grads_v))
    loads = [
        [
            pltpu.make_async_copy(source.at[cut], target.at[cut], sems.at[4 * i + j])
            for j, (source, target) in enumerate(arrays)
        ]
        for i, cut in enumerate(cuts)
    ]
    for load in loads:
        for copy in load:
            copy.start()

    def part(values, table, cut):
        matrix = ((2 * table[cut] - 1).astype(F32) * scale).astype(BF16)
        return lax.dot_general(
            values[cut], matrix, (((1,), (1,)), ((), ())), preferred_element_type=F32
        )

    x = g = jnp.zeros((tokens, rank), F32)
    for load, cut in zip(loads, cuts):
        for copy in load:
            copy.wait()
        x = x + part(acts_v, in_v, cut)
        g = g + part(grads_v, out_v, cut)
    both = jnp.concatenate([x, g], axis=1)
    left = lax.broadcasted_iota(jnp.int32, (rank, 2 * rank), 1) < rank
    total = jnp.zeros((rank, 2 * rank), F32)
    blocks = []
    for e in range(tokens // SEQ):
        rows = both[e * SEQ : (e + 1) * SEQ]
        gram = lax.dot_general(
            rows, rows, (((0,), (0,)), ((), ())), precision=HIGH, preferred_element_type=F32
        )
        total = total + jnp.where(left, gram[:rank], gram[rank:])
        blocks.append(gram[rank:, :rank])
    fac[...] = total
    outer[...] = jnp.concatenate(blocks, axis=1).astype(BF16)


def project(acts, grads, tab_in, tab_out):
    tokens, width = acts.shape
    rank = tab_in.shape[0]
    chunk = 256
    return pl.pallas_call(
        functools.partial(project_kernel, scale=1.0 / math.sqrt(width), chunk=chunk),
        in_specs=[pl.BlockSpec(memory_space=pl.ANY)] * 4,
        out_specs=[pl.BlockSpec(memory_space=pltpu.VMEM)] * 2,
        out_shape=[
            jax.ShapeDtypeStruct((rank, 2 * rank), F32),
            jax.ShapeDtypeStruct((rank, tokens // SEQ * rank), BF16),
        ],
        scratch_shapes=[
            pltpu.VMEM((tokens, width), BF16),
            pltpu.VMEM((tokens, width), BF16),
            pltpu.VMEM((rank, width), jnp.int32),
            pltpu.VMEM((rank, width), jnp.int32),
            pltpu.SemaphoreType.DMA((4 * width // chunk,)),
        ],
        compiler_params=pltpu.CompilerParams(vmem_limit_bytes=53 * 2**20 + 2**18),
        cost_estimate=pl.CostEstimate(
            flops=4 * tokens * width * rank, bytes_accessed=10 * 2**20, transcendentals=0
        ),
        name="project",
    )(acts, grads, tab_in, tab_out)


def solve_two(a, b, c, d, top, bottom):
    inv = 1.0 / (a * d - b * c)
    return (d * top - b * bottom) * inv, (a * bottom - c * top) * inv


def invert_pair(mat):
    rank = mat.shape[0]
    lane = lax.broadcasted_iota(jnp.int32, (1, 2 * rank), 1)
    row = lax.broadcasted_iota(jnp.int32, (rank, 1), 0)
    left = lane < rank
    place = lane & (rank - 1)
    for k in range(0, rank, 4):
        cols = [
            jnp.where(left, mat[:, k + i : k + i + 1], mat[:, rank + k + i : rank + k + i + 1])
            for i in range(4)
        ]
        m = [[cols[j][k + i : k + i + 1] for j in range(4)] for i in range(4)]
        rows = []
        for i in range(4):
            line = mat[k + i : k + i + 1]
            for j in range(4):
                line = jnp.where(place == k + j, 1.0 if i == j else 0.0, line)
            rows.append(line)
        head = m[0][0], m[0][1], m[1][0], m[1][1]
        u0, u1 = solve_two(*head, rows[0], rows[1])
        p0, p1 = solve_two(*head, m[0][2], m[1][2])
        q0, q1 = solve_two(*head, m[0][3], m[1][3])
        schur = (
            m[2][2] - m[2][0] * p0 - m[2][1] * p1,
            m[2][3] - m[2][0] * q0 - m[2][1] * q1,
            m[3][2] - m[3][0] * p0 - m[3][1] * p1,
            m[3][3] - m[3][0] * q0 - m[3][1] * q1,
        )
        t0 = rows[2] - m[2][0] * u0 - m[2][1] * u1
        t1 = rows[3] - m[3][0] * u0 - m[3][1] * u1
        v0, v1 = solve_two(*schur, t0, t1)
        solved = [u0 - p0 * v0 - q0 * v1, u1 - p1 * v0 - q1 * v1, v0, v1]
        rest = jnp.where((place >= k) & (place < k + 4), 0.0, mat)
        for i in range(4):
            rest = rest - cols[i] * solved[i]
        for i in range(4):
            rest = jnp.where(row == k + i, solved[i], rest)
        mat = rest
    return mat


def halves(value):
    hi = value.astype(BF16)
    return hi, (value - hi.astype(F32)).astype(BF16)


def invert_kernel(fac, out, *, tokens):
    rank = fac.shape[0]
    mat = fac[...] / tokens
    lane = lax.broadcasted_iota(jnp.int32, (rank, 2 * rank), 1)
    row = lax.broadcasted_iota(jnp.int32, (rank, 2 * rank), 0)
    left = lane < rank
    diag = jnp.where((lane & (rank - 1)) == row, mat, 0.0)
    ridge_in = DAMPING * jnp.sum(jnp.where(left, diag, 0.0), keepdims=True) / rank
    ridge_out = DAMPING * jnp.sum(jnp.where(left, 0.0, diag), keepdims=True) / rank
    ridge = jnp.where(left, ridge_in, ridge_out)
    out[...] = invert_pair(mat + jnp.where((lane & (rank - 1)) == row, ridge, 0.0))


def invert(fac, tokens):
    return pl.pallas_call(
        functools.partial(invert_kernel, tokens=tokens),
        out_shape=jax.ShapeDtypeStruct(fac.shape, F32),
        compiler_params=pltpu.CompilerParams(vmem_limit_bytes=4 * 2**20),
        cost_estimate=pl.CostEstimate(
            flops=25 * 10**8, bytes_accessed=2**16, transcendentals=0
        ),
        name="invert",
    )(fac)


def finish_kernel(layout, inverses, near, far, *refs):
    queries, (out, held, train, scores) = refs[:4], refs[4:]
    rank = inverses.shape[0]
    mat = inverses[...]
    inv_in = mat[:, :rank]
    inv_out = mat[:, rank:]
    out_hi, out_lo = halves(inv_out)
    four = 4 * rank
    rows4 = lax.broadcasted_iota(jnp.int32, (four, four), 0) // rank
    cols4 = lax.broadcasted_iota(jnp.int32, (four, four), 1) // rank
    tiled = jnp.concatenate([inv_in] * 4, axis=1)
    tiled = jnp.concatenate([tiled] * 4, axis=0)
    in_hi, in_lo = halves(jnp.where(rows4 == cols4, tiled, 0.0))
    dot = functools.partial(jnp.dot, preferred_element_type=F32)
    half = near.shape[0] // rank
    places = 2 * half
    wide = near.shape[1]
    for p in range(places):
        at = p % half * rank
        part = (near if p < half else far)[at : at + rank, :]
        first = dot(out_hi, part) + dot(out_lo, part)
        hi, lo = halves(first)
        for c in range(wide // four):
            cut = slice(c * four, (c + 1) * four)
            held[p, :, cut] = dot(hi[:, cut], in_hi) + (
                dot(hi[:, cut], in_lo) + dot(lo[:, cut], in_hi)
            )
    low = lax.broadcasted_iota(jnp.int32, (places, 2 * rank), 1) < rank
    for o in range(0, rank, 2):
        even = held[:, o, :]
        odd = held[:, o + 1, :]
        pieces = []
        for pair in range(wide // (2 * rank)):
            cut = slice(pair * 2 * rank, (pair + 1) * 2 * rank)
            a, b = even[:, cut], odd[:, cut]
            pieces.append(jnp.where(low, a, pltpu.roll(b, rank, 1)))
            pieces.append(jnp.where(low, pltpu.roll(a, rank, 1), b))
        train[:, o * rank : (o + 2) * rank] = jnp.concatenate(pieces, axis=0).astype(BF16)
    nt = (((1,), (1,)), ((), ()))
    for i in range(2):
        parts = [
            lax.dot_general(train[...], block[...], nt, preferred_element_type=F32)
            for block in queries[2 * i : 2 * i + 2]
        ]
        scores[i] = jnp.concatenate(parts, axis=1)
    examples = wide // rank
    rows_out = examples // 2
    run = scores.shape[2] // 4
    for p in range(places):
        for i in range(2):
            rows = scores[i, pl.ds(p, examples, places), :]
            for j in range(2):
                pair = rows[:, 2 * j * run : 2 * (j + 1) * run]
                turned = jnp.concatenate([pair[:, run:], pair[:, :run]], axis=1)
                cut = jnp.where(layout[places + 4 + j] == 1, turned, pair)
                target = layout[p] * 4 + layout[places + 2 * i + j]
                out[target] = jnp.concatenate([cut[:rows_out], cut[rows_out:]], axis=1)


def finish(layout, inverses, near, far, queries):
    rank = inverses.shape[0]
    places = 2 * near.shape[0] // rank
    examples = near.shape[1] // rank
    count = queries[0].shape[0]
    return pl.pallas_call(
        finish_kernel,
        out_shape=jax.ShapeDtypeStruct((places * 4, examples // 2, 2 * count), F32),
        in_specs=[pl.BlockSpec(memory_space=pltpu.SMEM)]
        + [pl.BlockSpec(memory_space=pltpu.VMEM)] * 7,
        scratch_shapes=[
            pltpu.VMEM((places, rank, near.shape[1]), F32),
            pltpu.VMEM((places * examples, rank * rank), BF16),
            pltpu.VMEM((2, places * examples, 2 * count), F32),
        ],
        compiler_params=pltpu.CompilerParams(vmem_limit_bytes=16 * 2**20),
        cost_estimate=pl.CostEstimate(
            flops=40 * 10**8, bytes_accessed=2**20, transcendentals=0
        ),
        name="finish",
    )(layout, inverses, near, far, *queries)


def collect_kernel(parts, out, *, groups):
    places = parts.shape[0] // groups
    half, wide = parts.shape[1], parts.shape[2] // 2
    runs = wide // 2
    tops, bottoms = [], []
    for p in range(places):
        total = parts[p * groups]
        for g in range(1, groups):
            total = total + parts[p * groups + g]
        tops.append(total[:, :wide])
        bottoms.append(total[:, wide:])
    for rows, cuts in ((0, tops), (half, bottoms)):
        line = [cut[:, r * runs : (r + 1) * runs] for r in range(2) for cut in cuts]
        out[rows : rows + half, :] = jnp.concatenate(line, axis=1)


def collect(parts, groups):
    places = parts.shape[0] // groups
    return pl.pallas_call(
        functools.partial(collect_kernel, groups=groups),
        out_shape=jax.ShapeDtypeStruct(
            (2 * parts.shape[1], places * parts.shape[2] // 2), F32
        ),
        compiler_params=pltpu.CompilerParams(vmem_limit_bytes=4 * 2**20),
        name="collect",
    )(parts)


def per_device(acts, out_grads, proj_in, proj_out, query_grads):
    groups = lax.axis_size(("yh", "core"))
    tie = lax.optimization_barrier
    own = query_grads[0]
    got = swap(own, "x", RING4[0])
    layout = jnp.asarray(layouts())[
        lax.axis_index("yl"), lax.axis_index("x"), lax.axis_index("z")
    ]
    fac, outer = project(acts[0], out_grads[0], proj_in[0], proj_out[0])
    seen = swap(outer, "z", RING8[0])
    fac = fac + swap(fac, "yl", PAIR)
    fac, own, got = tie((fac, own, got))
    first = join(own, got, 20 * 10**8)
    second = swap(first, "x", RING4[1])
    fac = fac + swap(fac, "z", RING8_LAST[0])
    fac, first, outer, seen = tie((fac, first, outer, seen))
    third = swap(first, "yl", PAIR)
    outer = join(outer, seen, 60 * 10**8)
    seen = swap(outer, "z", RING8[1])
    fac = fac + swap(fac, "z", RING8_LAST[1])
    fac = fac + swap(fac, "z", RING8_LAST[2])
    fac, outer, seen, second, third = tie((fac, outer, seen, second, third))
    outer = join(outer, seen, 60 * 10**8)
    seen = swap(outer, "z", RING8[2])
    fourth = swap(second, "yl", PAIR)
    fac = fac + swap(fac, "x", RING4[0])
    fac = fac + swap(fac, "x", RING4[1])
    tokens = acts.shape[1] * lax.axis_size(("yl", "x", "z"))
    inverses = invert(fac, tokens)
    inverses, outer, seen = tie((inverses, outer, seen))
    parts = finish(layout, inverses, outer, seen, (first, second, third, fourth))
    parts = lax.all_to_all(parts, ("z", "yh", "core"), 0, 0, tiled=True)
    return collect(parts, groups).T


def solution(mesh):
    split = Mesh(mesh.devices.reshape(2, 4, 8, 2, 2), ("yl", "x", "z", "yh", "core"))
    dp, grp = ("yl", "x", "z"), ("yh", "core")
    return jax.shard_map(
        per_device,
        mesh=split,
        in_specs=(
            P(grp, dp, None),
            P(grp, dp, None),
            P(grp, None, None),
            P(grp, None, None),
            P(grp, dp, None),
        ),
        out_specs=P(grp, dp),
        check_vma=False,
    )
```

```python
import functools
import math

import jax
import jax.numpy as jnp
import numpy as np
from jax import lax
from jax.experimental import pallas as pl
from jax.experimental.pallas import tpu as pltpu
from jax.sharding import Mesh, PartitionSpec as P

SEQ = 64
DAMPING = 0.1
HIGH = lax.Precision.HIGHEST
F32 = jnp.float32
BF16 = jnp.bfloat16

PAIR = [(0, 1)]
RING4 = [[(0, 1), (2, 3)], [(1, 2), (3, 0)]]
RING8 = [
    [(0, 5), (1, 4), (2, 7), (3, 6)],
    [(0, 1), (2, 3), (4, 5), (6, 7)],
    [(1, 2), (3, 4), (5, 6), (7, 0)],
]

RING8_LAST = [RING8[1], RING8[2], [(1, 6), (2, 5), (0, 3), (7, 4)]]


def swap(value, axis, pairs):
    return lax.ppermute(value, axis, pairs + [(b, a) for a, b in pairs])


def gathered(rings, size):
    held = [[z] for z in range(size)]
    for pairs in rings:
        partner = {}
        for a, b in pairs:
            partner[a], partner[b] = b, a
        held = [held[z] + held[partner[z]] for z in range(size)]
    return held


def join_kernel(a, b, out):
    rows = a.shape[0]
    out[:rows, :] = a[...]
    out[rows:, :] = b[...]


def join(a, b, work):
    return pl.pallas_call(
        join_kernel,
        out_shape=jax.ShapeDtypeStruct((2 * a.shape[0], a.shape[1]), a.dtype),
        compiler_params=pltpu.CompilerParams(vmem_limit_bytes=4 * 2**20),
        cost_estimate=pl.CostEstimate(flops=work, bytes_accessed=2**20, transcendentals=0),
        name="join",
    )(a, b)


def layouts():
    trains, pairs = gathered(RING8, 8), gathered(RING4, 4)
    table = np.zeros((2, 4, 8, 16), np.int32)
    for y, x, z in np.ndindex(2, 4, 8):
        at = pairs[x]
        groups = [(y ^ i) * 2 + at[2 * j] // 2 for i in range(2) for j in range(2)]
        table[y, x, z, :14] = trains[z] + groups + [at[0] % 2, at[2] % 2]
    return table


def project_kernel(
    acts, grads, tab_in, tab_out, fac, outer, acts_v, grads_v, in_v, out_v, sems, *, scale, chunk
):
    tokens, width = acts.shape
    rank = tab_in.shape[0]
    cuts = [(slice(None), pl.ds(at, chunk)) for at in range(0, width, chunk)]
    arrays = ((tab_in, in_v), (tab_out, out_v), (acts, acts_v), (grads, grads_v))
    loads = [
        [
            pltpu.make_async_copy(source.at[cut], target.at[cut], sems.at[4 * i + j])
            for j, (source, target) in enumerate(arrays)
        ]
        for i, cut in enumerate(cuts)
    ]
    for load in loads:
        for copy in load:
            copy.start()

    def part(values, table, cut):
        matrix = ((2 * table[cut] - 1).astype(F32) * scale).astype(BF16)
        return lax.dot_general(
            values[cut], matrix, (((1,), (1,)), ((), ())), preferred_element_type=F32
        )

    x = g = jnp.zeros((tokens, rank), F32)
    for load, cut in zip(loads, cuts):
        for copy in load:
            copy.wait()
        x = x + part(acts_v, in_v, cut)
        g = g + part(grads_v, out_v, cut)
    both = jnp.concatenate([x, g], axis=1)
    left = lax.broadcasted_iota(jnp.int32, (rank, 2 * rank), 1) < rank
    total = jnp.zeros((rank, 2 * rank), F32)
    blocks = []
    for e in range(tokens // SEQ):
        rows = both[e * SEQ : (e + 1) * SEQ]
        gram = lax.dot_general(
            rows, rows, (((0,), (0,)), ((), ())), precision=HIGH, preferred_element_type=F32
        )
        total = total + jnp.where(left, gram[:rank], gram[rank:])
        blocks.append(gram[rank:, :rank])
    fac[...] = total
    outer[...] = jnp.concatenate(blocks, axis=1).astype(BF16)


def project(acts, grads, tab_in, tab_out):
    tokens, width = acts.shape
    rank = tab_in.shape[0]
    chunk = 256
    return pl.pallas_call(
        functools.partial(project_kernel, scale=1.0 / math.sqrt(width), chunk=chunk),
        in_specs=[pl.BlockSpec(memory_space=pl.ANY)] * 4,
        out_specs=[pl.BlockSpec(memory_space=pltpu.VMEM)] * 2,
        out_shape=[
            jax.ShapeDtypeStruct((rank, 2 * rank), F32),
            jax.ShapeDtypeStruct((rank, tokens // SEQ * rank), BF16),
        ],
        scratch_shapes=[
            pltpu.VMEM((tokens, width), BF16),
            pltpu.VMEM((tokens, width), BF16),
            pltpu.VMEM((rank, width), jnp.int32),
            pltpu.VMEM((rank, width), jnp.int32),
            pltpu.SemaphoreType.DMA((4 * width // chunk,)),
        ],
        compiler_params=pltpu.CompilerParams(vmem_limit_bytes=53 * 2**20 + 2**18),
        cost_estimate=pl.CostEstimate(
            flops=4 * tokens * width * rank, bytes_accessed=10 * 2**20, transcendentals=0
        ),
        name="project",
    )(acts, grads, tab_in, tab_out)


def solve_two(a, b, c, d, top, bottom):
    inv = 1.0 / (a * d - b * c)
    return (d * top - b * bottom) * inv, (a * bottom - c * top) * inv


def invert_pair(mat):
    rank = mat.shape[0]
    lane = lax.broadcasted_iota(jnp.int32, (1, 2 * rank), 1)
    row = lax.broadcasted_iota(jnp.int32, (rank, 1), 0)
    left = lane < rank
    place = lane & (rank - 1)
    for k in range(0, rank, 4):
        cols = [
            jnp.where(left, mat[:, k + i : k + i + 1], mat[:, rank + k + i : rank + k + i + 1])
            for i in range(4)
        ]
        m = [[cols[j][k + i : k + i + 1] for j in range(4)] for i in range(4)]
        rows = []
        for i in range(4):
            line = mat[k + i : k + i + 1]
            for j in range(4):
                line = jnp.where(place == k + j, 1.0 if i == j else 0.0, line)
            rows.append(line)
        head = m[0][0], m[0][1], m[1][0], m[1][1]
        u0, u1 = solve_two(*head, rows[0], rows[1])
        p0, p1 = solve_two(*head, m[0][2], m[1][2])
        q0, q1 = solve_two(*head, m[0][3], m[1][3])
        schur = (
            m[2][2] - m[2][0] * p0 - m[2][1] * p1,
            m[2][3] - m[2][0] * q0 - m[2][1] * q1,
            m[3][2] - m[3][0] * p0 - m[3][1] * p1,
            m[3][3] - m[3][0] * q0 - m[3][1] * q1,
        )
        t0 = rows[2] - m[2][0] * u0 - m[2][1] * u1
        t1 = rows[3] - m[3][0] * u0 - m[3][1] * u1
        v0, v1 = solve_two(*schur, t0, t1)
        solved = [u0 - p0 * v0 - q0 * v1, u1 - p1 * v0 - q1 * v1, v0, v1]
        rest = jnp.where((place >= k) & (place < k + 4), 0.0, mat)
        for i in range(4):
            rest = rest - cols[i] * solved[i]
        for i in range(4):
            rest = jnp.where(row == k + i, solved[i], rest)
        mat = rest
    return mat


def halves(value):
    hi = value.astype(BF16)
    return hi, (value - hi.astype(F32)).astype(BF16)


def invert_kernel(fac, out, *, tokens):
    rank = fac.shape[0]
    mat = fac[...] / tokens
    lane = lax.broadcasted_iota(jnp.int32, (rank, 2 * rank), 1)
    row = lax.broadcasted_iota(jnp.int32, (rank, 2 * rank), 0)
    left = lane < rank
    diag = jnp.where((lane & (rank - 1)) == row, mat, 0.0)
    ridge_in = DAMPING * jnp.sum(jnp.where(left, diag, 0.0), keepdims=True) / rank
    ridge_out = DAMPING * jnp.sum(jnp.where(left, 0.0, diag), keepdims=True) / rank
    ridge = jnp.where(left, ridge_in, ridge_out)
    out[...] = invert_pair(mat + jnp.where((lane & (rank - 1)) == row, ridge, 0.0))


def invert(fac, tokens):
    return pl.pallas_call(
        functools.partial(invert_kernel, tokens=tokens),
        out_shape=jax.ShapeDtypeStruct(fac.shape, F32),
        compiler_params=pltpu.CompilerParams(vmem_limit_bytes=4 * 2**20),
        cost_estimate=pl.CostEstimate(
            flops=25 * 10**8, bytes_accessed=2**16, transcendentals=0
        ),
        name="invert",
    )(fac)


def finish_kernel(layout, inverses, near, far, *refs):
    queries, (out, held, train, scores, his, los) = refs[:4], refs[4:]
    rank = inverses.shape[0]
    mat = inverses[...]
    inv_in = mat[:, :rank]
    inv_out = mat[:, rank:]
    out_hi, out_lo = halves(inv_out)
    four = 4 * rank
    rows4 = lax.broadcasted_iota(jnp.int32, (four, four), 0) // rank
    cols4 = lax.broadcasted_iota(jnp.int32, (four, four), 1) // rank
    tiled = jnp.concatenate([inv_in] * 4, axis=1)
    tiled = jnp.concatenate([tiled] * 4, axis=0)
    in_hi, in_lo = halves(jnp.where(rows4 == cols4, tiled, 0.0))
    dot = functools.partial(jnp.dot, preferred_element_type=F32)
    half = near.shape[0] // rank
    places = 2 * half
    wide = near.shape[1]
    out_both = jnp.concatenate([out_hi, out_lo], axis=0)
    for p in range(places):
        at = p % half * rank
        both = dot(out_both, (near if p < half else far)[at : at + rank, :])
        hi, lo = halves(both[:rank] + both[rank:])
        his[p * rank : (p + 1) * rank, :] = hi
        los[p * rank : (p + 1) * rank, :] = lo
    for c in range(wide // four):
        cut = slice(c * four, (c + 1) * four)
        second = dot(his[:, cut], in_hi) + (dot(his[:, cut], in_lo) + dot(los[:, cut], in_hi))
        held[:, :, cut] = second.reshape(places, rank, four)
    low = lax.broadcasted_iota(jnp.int32, (places, 2 * rank), 1) < rank
    for o in range(0, rank, 2):
        even = held[:, o, :]
        odd = held[:, o + 1, :]
        pieces = []
        for pair in range(wide // (2 * rank)):
            cut = slice(pair * 2 * rank, (pair + 1) * 2 * rank)
            a, b = even[:, cut], odd[:, cut]
            pieces.append(jnp.where(low, a, pltpu.roll(b, rank, 1)))
            pieces.append(jnp.where(low, pltpu.roll(a, rank, 1), b))
        train[:, o * rank : (o + 2) * rank] = jnp.concatenate(pieces, axis=0).astype(BF16)
    nt = (((1,), (1,)), ((), ()))
    for i in range(2):
        parts = [
            lax.dot_general(train[...], block[...], nt, preferred_element_type=F32)
            for block in queries[2 * i : 2 * i + 2]
        ]
        scores[i] = jnp.concatenate(parts, axis=1)
    examples = wide // rank
    rows_out = examples // 2
    run = scores.shape[2] // 4
    for p in range(places):
        for i in range(2):
            rows = scores[i, pl.ds(p, examples, places), :]
            for j in range(2):
                pair = rows[:, 2 * j * run : 2 * (j + 1) * run]
                turned = jnp.concatenate([pair[:, run:], pair[:, :run]], axis=1)
                cut = jnp.where(layout[places + 4 + j] == 1, turned, pair)
                target = layout[p] * 4 + layout[places + 2 * i + j]
                out[target] = jnp.concatenate([cut[:rows_out], cut[rows_out:]], axis=1)


def finish(layout, inverses, near, far, queries):
    rank = inverses.shape[0]
    places = 2 * near.shape[0] // rank
    examples = near.shape[1] // rank
    count = queries[0].shape[0]
    return pl.pallas_call(
        finish_kernel,
        out_shape=jax.ShapeDtypeStruct((places * 4, examples // 2, 2 * count), F32),
        in_specs=[pl.BlockSpec(memory_space=pltpu.SMEM)]
        + [pl.BlockSpec(memory_space=pltpu.VMEM)] * 7,
        scratch_shapes=[
            pltpu.VMEM((places, rank, near.shape[1]), F32),
            pltpu.VMEM((places * examples, rank * rank), BF16),
            pltpu.VMEM((2, places * examples, 2 * count), F32),
            pltpu.VMEM((places * rank, near.shape[1]), BF16),
            pltpu.VMEM((places * rank, near.shape[1]), BF16),
        ],
        compiler_params=pltpu.CompilerParams(vmem_limit_bytes=16 * 2**20),
        cost_estimate=pl.CostEstimate(
            flops=40 * 10**8, bytes_accessed=2**20, transcendentals=0
        ),
        name="finish",
    )(layout, inverses, near, far, *queries)


def collect_kernel(parts, out, *, groups):
    places = parts.shape[0] // groups
    half, wide = parts.shape[1], parts.shape[2] // 2
    runs = wide // 2
    tops, bottoms = [], []
    for p in range(places):
        total = parts[p * groups]
        for g in range(1, groups):
            total = total + parts[p * groups + g]
        tops.append(total[:, :wide])
        bottoms.append(total[:, wide:])
    for rows, cuts in ((0, tops), (half, bottoms)):
        line = [cut[:, r * runs : (r + 1) * runs] for r in range(2) for cut in cuts]
        out[rows : rows + half, :] = jnp.concatenate(line, axis=1)


def collect(parts, groups):
    places = parts.shape[0] // groups
    return pl.pallas_call(
        functools.partial(collect_kernel, groups=groups),
        out_shape=jax.ShapeDtypeStruct(
            (2 * parts.shape[1], places * parts.shape[2] // 2), F32
        ),
        compiler_params=pltpu.CompilerParams(vmem_limit_bytes=4 * 2**20),
        name="collect",
    )(parts)


def per_device(acts, out_grads, proj_in, proj_out, query_grads):
    groups = lax.axis_size(("yh", "core"))
    tie = lax.optimization_barrier
    own = query_grads[0]
    got = swap(own, "x", RING4[0])
    layout = jnp.asarray(layouts())[
        lax.axis_index("yl"), lax.axis_index("x"), lax.axis_index("z")
    ]
    fac, outer = project(acts[0], out_grads[0], proj_in[0], proj_out[0])
    seen = swap(outer, "z", RING8[0])
    fac = fac + swap(fac, "yl", PAIR)
    fac, own, got = tie((fac, own, got))
    first = join(own, got, 20 * 10**8)
    second = swap(first, "x", RING4[1])
    fac = fac + swap(fac, "z", RING8_LAST[0])
    fac, first, outer, seen = tie((fac, first, outer, seen))
    third = swap(first, "yl", PAIR)
    outer = join(outer, seen, 60 * 10**8)
    seen = swap(outer, "z", RING8[1])
    fac = fac + swap(fac, "z", RING8_LAST[1])
    fac = fac + swap(fac, "z", RING8_LAST[2])
    fac, outer, seen, second, third = tie((fac, outer, seen, second, third))
    outer = join(outer, seen, 60 * 10**8)
    seen = swap(outer, "z", RING8[2])
    fourth = swap(second, "yl", PAIR)
    fac = fac + swap(fac, "x", RING4[0])
    fac = fac + swap(fac, "x", RING4[1])
    tokens = acts.shape[1] * lax.axis_size(("yl", "x", "z"))
    inverses = invert(fac, tokens)
    inverses, outer, seen = tie((inverses, outer, seen))
    parts = finish(layout, inverses, outer, seen, (first, second, third, fourth))
    parts = lax.all_to_all(parts, ("z", "yh", "core"), 0, 0, tiled=True)
    return collect(parts, groups).T


def solution(mesh):
    split = Mesh(mesh.devices.reshape(2, 4, 8, 2, 2), ("yl", "x", "z", "yh", "core"))
    dp, grp = ("yl", "x", "z"), ("yh", "core")
    return jax.shard_map(
        per_device,
        mesh=split,
        in_specs=(
            P(grp, dp, None),
            P(grp, dp, None),
            P(grp, None, None),
            P(grp, None, None),
            P(grp, dp, None),
        ),
        out_specs=P(grp, dp),
        check_vma=False,
    )
```

```python
import functools
import math

import jax
import jax.numpy as jnp
import numpy as np
from jax import lax
from jax.experimental import pallas as pl
from jax.experimental.pallas import tpu as pltpu
from jax.sharding import Mesh, PartitionSpec as P

SEQ = 64
DAMPING = 0.1
HIGH = lax.Precision.HIGHEST
F32 = jnp.float32
BF16 = jnp.bfloat16

PAIR = [(0, 1)]
RING4 = [[(0, 1), (2, 3)], [(1, 2), (3, 0)]]
RING8 = [
    [(0, 5), (1, 4), (2, 7), (3, 6)],
    [(0, 1), (2, 3), (4, 5), (6, 7)],
    [(1, 2), (3, 4), (5, 6), (7, 0)],
]

RING8_LAST = [RING8[1], RING8[2], [(1, 6), (2, 5), (0, 3), (7, 4)]]


def swap(value, axis, pairs):
    return lax.ppermute(value, axis, pairs + [(b, a) for a, b in pairs])


def gathered(rings, size):
    held = [[z] for z in range(size)]
    for pairs in rings:
        partner = {}
        for a, b in pairs:
            partner[a], partner[b] = b, a
        held = [held[z] + held[partner[z]] for z in range(size)]
    return held


def join_kernel(a, b, out):
    rows = a.shape[0]
    out[:rows, :] = a[...]
    out[rows:, :] = b[...]


def join(a, b, work):
    return pl.pallas_call(
        join_kernel,
        out_shape=jax.ShapeDtypeStruct((2 * a.shape[0], a.shape[1]), a.dtype),
        compiler_params=pltpu.CompilerParams(vmem_limit_bytes=4 * 2**20),
        cost_estimate=pl.CostEstimate(flops=work, bytes_accessed=2**20, transcendentals=0),
        name="join",
    )(a, b)


def layouts():
    trains, pairs = gathered(RING8, 8), gathered(RING4, 4)
    table = np.zeros((2, 4, 8, 16), np.int32)
    for y, x, z in np.ndindex(2, 4, 8):
        at = pairs[x]
        groups = [(y ^ i) * 2 + at[2 * j] // 2 for i in range(2) for j in range(2)]
        table[y, x, z, :14] = trains[z] + groups + [at[0] % 2, at[2] % 2]
    return table


def project_kernel(
    acts, grads, tab_in, tab_out, fac, outer, acts_v, grads_v, in_v, out_v, sems, *, scale, chunk
):
    tokens, width = acts.shape
    rank = tab_in.shape[0]
    cuts = [(slice(None), pl.ds(at, chunk)) for at in range(0, width, chunk)]
    arrays = ((tab_in, in_v), (tab_out, out_v), (acts, acts_v), (grads, grads_v))
    loads = [
        [
            pltpu.make_async_copy(source.at[cut], target.at[cut], sems.at[4 * i + j])
            for j, (source, target) in enumerate(arrays)
        ]
        for i, cut in enumerate(cuts)
    ]
    for load in loads:
        for copy in load:
            copy.start()

    def part(values, table, cut):
        matrix = ((2 * table[cut] - 1).astype(F32) * scale).astype(BF16)
        return lax.dot_general(
            values[cut], matrix, (((1,), (1,)), ((), ())), preferred_element_type=F32
        )

    x = g = jnp.zeros((tokens, rank), F32)
    for load, cut in zip(loads, cuts):
        for copy in load:
            copy.wait()
        x = x + part(acts_v, in_v, cut)
        g = g + part(grads_v, out_v, cut)
    both = jnp.concatenate([x, g], axis=1)
    left = lax.broadcasted_iota(jnp.int32, (rank, 2 * rank), 1) < rank
    total = jnp.zeros((rank, 2 * rank), F32)
    blocks = []
    for e in range(tokens // SEQ):
        rows = both[e * SEQ : (e + 1) * SEQ]
        gram = lax.dot_general(
            rows, rows, (((0,), (0,)), ((), ())), precision=HIGH, preferred_element_type=F32
        )
        total = total + jnp.where(left, gram[:rank], gram[rank:])
        blocks.append(gram[rank:, :rank])
    fac[...] = total
    outer[...] = jnp.concatenate(blocks, axis=1).astype(BF16)


def project(acts, grads, tab_in, tab_out):
    tokens, width = acts.shape
    rank = tab_in.shape[0]
    chunk = 256
    return pl.pallas_call(
        functools.partial(project_kernel, scale=1.0 / math.sqrt(width), chunk=chunk),
        in_specs=[pl.BlockSpec(memory_space=pl.ANY)] * 4,
        out_specs=[pl.BlockSpec(memory_space=pltpu.VMEM)] * 2,
        out_shape=[
            jax.ShapeDtypeStruct((rank, 2 * rank), F32),
            jax.ShapeDtypeStruct((rank, tokens // SEQ * rank), BF16),
        ],
        scratch_shapes=[
            pltpu.VMEM((tokens, width), BF16),
            pltpu.VMEM((tokens, width), BF16),
            pltpu.VMEM((rank, width), jnp.int32),
            pltpu.VMEM((rank, width), jnp.int32),
            pltpu.SemaphoreType.DMA((4 * width // chunk,)),
        ],
        compiler_params=pltpu.CompilerParams(vmem_limit_bytes=53 * 2**20 + 2**18),
        cost_estimate=pl.CostEstimate(
            flops=4 * tokens * width * rank, bytes_accessed=10 * 2**20, transcendentals=0
        ),
        name="project",
    )(acts, grads, tab_in, tab_out)


def solve_two(a, b, c, d, top, bottom):
    inv = 1.0 / (a * d - b * c)
    return (d * top - b * bottom) * inv, (a * bottom - c * top) * inv


def invert_pair(mat):
    rank = mat.shape[0]
    lane = lax.broadcasted_iota(jnp.int32, (1, 2 * rank), 1)
    row = lax.broadcasted_iota(jnp.int32, (rank, 1), 0)
    left = lane < rank
    place = lane & (rank - 1)
    for k in range(0, rank, 4):
        cols = [
            jnp.where(left, mat[:, k + i : k + i + 1], mat[:, rank + k + i : rank + k + i + 1])
            for i in range(4)
        ]
        m = [[cols[j][k + i : k + i + 1] for j in range(4)] for i in range(4)]
        rows = []
        for i in range(4):
            line = mat[k + i : k + i + 1]
            for j in range(4):
                line = jnp.where(place == k + j, 1.0 if i == j else 0.0, line)
            rows.append(line)
        head = m[0][0], m[0][1], m[1][0], m[1][1]
        u0, u1 = solve_two(*head, rows[0], rows[1])
        p0, p1 = solve_two(*head, m[0][2], m[1][2])
        q0, q1 = solve_two(*head, m[0][3], m[1][3])
        schur = (
            m[2][2] - m[2][0] * p0 - m[2][1] * p1,
            m[2][3] - m[2][0] * q0 - m[2][1] * q1,
            m[3][2] - m[3][0] * p0 - m[3][1] * p1,
            m[3][3] - m[3][0] * q0 - m[3][1] * q1,
        )
        t0 = rows[2] - m[2][0] * u0 - m[2][1] * u1
        t1 = rows[3] - m[3][0] * u0 - m[3][1] * u1
        v0, v1 = solve_two(*schur, t0, t1)
        solved = [u0 - p0 * v0 - q0 * v1, u1 - p1 * v0 - q1 * v1, v0, v1]
        rest = jnp.where((place >= k) & (place < k + 4), 0.0, mat)
        for i in range(4):
            rest = rest - cols[i] * solved[i]
        for i in range(4):
            rest = jnp.where(row == k + i, solved[i], rest)
        mat = rest
    return mat


def halves(value):
    hi = value.astype(BF16)
    return hi, (value - hi.astype(F32)).astype(BF16)


def invert_kernel(fac, out, *, tokens):
    rank = fac.shape[0]
    mat = fac[...] / tokens
    lane = lax.broadcasted_iota(jnp.int32, (rank, 2 * rank), 1)
    row = lax.broadcasted_iota(jnp.int32, (rank, 2 * rank), 0)
    left = lane < rank
    diag = jnp.where((lane & (rank - 1)) == row, mat, 0.0)
    ridge_in = DAMPING * jnp.sum(jnp.where(left, diag, 0.0), keepdims=True) / rank
    ridge_out = DAMPING * jnp.sum(jnp.where(left, 0.0, diag), keepdims=True) / rank
    ridge = jnp.where(left, ridge_in, ridge_out)
    out[...] = invert_pair(mat + jnp.where((lane & (rank - 1)) == row, ridge, 0.0))


def invert(fac, tokens):
    return pl.pallas_call(
        functools.partial(invert_kernel, tokens=tokens),
        out_shape=jax.ShapeDtypeStruct(fac.shape, F32),
        compiler_params=pltpu.CompilerParams(vmem_limit_bytes=4 * 2**20),
        cost_estimate=pl.CostEstimate(
            flops=25 * 10**8, bytes_accessed=2**16, transcendentals=0
        ),
        name="invert",
    )(fac)


def finish_kernel(layout, inverses, near, far, *refs):
    queries, (out, held, train, scores, his, los) = refs[:4], refs[4:]
    rank = inverses.shape[0]
    mat = inverses[...]
    inv_in = mat[:, :rank]
    inv_out = mat[:, rank:]
    out_hi, out_lo = halves(inv_out)
    four = 4 * rank
    rows4 = lax.broadcasted_iota(jnp.int32, (four, four), 0) // rank
    cols4 = lax.broadcasted_iota(jnp.int32, (four, four), 1) // rank
    tiled = jnp.concatenate([inv_in] * 4, axis=1)
    tiled = jnp.concatenate([tiled] * 4, axis=0)
    in_hi, in_lo = halves(jnp.where(rows4 == cols4, tiled, 0.0))
    dot = functools.partial(jnp.dot, preferred_element_type=F32)
    half = near.shape[0] // rank
    places = 2 * half
    wide = near.shape[1]
    out_both = jnp.concatenate([out_hi, out_lo], axis=0)
    for p in range(places):
        at = p % half * rank
        both = dot(out_both, (near if p < half else far)[at : at + rank, :])
        hi, lo = halves(both[:rank] + both[rank:])
        his[p * rank : (p + 1) * rank, :] = hi
        los[p * rank : (p + 1) * rank, :] = lo
    for c in range(wide // four):
        cut = slice(c * four, (c + 1) * four)
        second = dot(his[:, cut], in_hi) + (dot(his[:, cut], in_lo) + dot(los[:, cut], in_hi))
        held[:, :, cut] = second.reshape(places, rank, four)
    low = lax.broadcasted_iota(jnp.int32, (places, 2 * rank), 1) < rank
    for o in range(0, rank, 2):
        even = held[:, o, :]
        odd = held[:, o + 1, :]
        pieces = []
        for pair in range(wide // (2 * rank)):
            cut = slice(pair * 2 * rank, (pair + 1) * 2 * rank)
            a, b = even[:, cut], odd[:, cut]
            pieces.append(jnp.where(low, a, pltpu.roll(b, rank, 1)))
            pieces.append(jnp.where(low, pltpu.roll(a, rank, 1), b))
        train[:, o * rank : (o + 2) * rank] = jnp.concatenate(pieces, axis=0).astype(BF16)
    nt = (((1,), (1,)), ((), ()))
    for i in range(2):
        parts = [
            lax.dot_general(train[...], block[...], nt, preferred_element_type=F32)
            for block in queries[2 * i : 2 * i + 2]
        ]
        scores[i] = jnp.concatenate(parts, axis=1)
    examples = wide // rank
    rows_out = examples // 2
    run = scores.shape[2] // 4
    for p in range(places):
        for i in range(2):
            rows = scores[i, pl.ds(p, examples, places), :]
            for j in range(2):
                pair = rows[:, 2 * j * run : 2 * (j + 1) * run]
                turned = jnp.concatenate([pair[:, run:], pair[:, :run]], axis=1)
                cut = jnp.where(layout[places + 4 + j] == 1, turned, pair)
                target = layout[p] * 4 + layout[places + 2 * i + j]
                out[target] = jnp.concatenate([cut[:rows_out], cut[rows_out:]], axis=1)


def finish(layout, inverses, near, far, queries):
    rank = inverses.shape[0]
    places = 2 * near.shape[0] // rank
    examples = near.shape[1] // rank
    count = queries[0].shape[0]
    return pl.pallas_call(
        finish_kernel,
        out_shape=jax.ShapeDtypeStruct((places * 4, examples // 2, 2 * count), F32),
        in_specs=[pl.BlockSpec(memory_space=pltpu.SMEM)]
        + [pl.BlockSpec(memory_space=pltpu.VMEM)] * 7,
        scratch_shapes=[
            pltpu.VMEM((places, rank, near.shape[1]), F32),
            pltpu.VMEM((places * examples, rank * rank), BF16),
            pltpu.VMEM((2, places * examples, 2 * count), F32),
            pltpu.VMEM((places * rank, near.shape[1]), BF16),
            pltpu.VMEM((places * rank, near.shape[1]), BF16),
        ],
        compiler_params=pltpu.CompilerParams(vmem_limit_bytes=16 * 2**20),
        cost_estimate=pl.CostEstimate(
            flops=40 * 10**8, bytes_accessed=2**20, transcendentals=0
        ),
        name="finish",
    )(layout, inverses, near, far, *queries)


def collect_kernel(parts, out, *, groups):
    places = parts.shape[0] // groups
    half, wide = parts.shape[1], parts.shape[2] // 2
    runs = wide // 2
    tops, bottoms = [], []
    for p in range(places):
        total = parts[p * groups]
        for g in range(1, groups):
            total = total + parts[p * groups + g]
        tops.append(total[:, :wide])
        bottoms.append(total[:, wide:])
    for rows, cuts in ((0, tops), (half, bottoms)):
        line = [cut[:, r * runs : (r + 1) * runs] for r in range(2) for cut in cuts]
        out[rows : rows + half, :] = jnp.concatenate(line, axis=1)


def collect(parts, groups):
    places = parts.shape[0] // groups
    return pl.pallas_call(
        functools.partial(collect_kernel, groups=groups),
        out_shape=jax.ShapeDtypeStruct(
            (2 * parts.shape[1], places * parts.shape[2] // 2), F32
        ),
        compiler_params=pltpu.CompilerParams(vmem_limit_bytes=4 * 2**20),
        name="collect",
    )(parts)


def per_device(acts, out_grads, proj_in, proj_out, query_grads):
    groups = lax.axis_size(("yh", "core"))
    tie = lax.optimization_barrier
    own = query_grads[0]
    got = swap(own, "x", RING4[0])
    layout = jnp.asarray(layouts())[
        lax.axis_index("yl"), lax.axis_index("x"), lax.axis_index("z")
    ]
    fac, outer = project(acts[0], out_grads[0], proj_in[0], proj_out[0])
    seen = swap(outer, "z", RING8[0])
    fac = fac + swap(fac, "yl", PAIR)
    fac, own, got = tie((fac, own, got))
    first = join(own, got, 1 * 10**8)
    second = swap(first, "x", RING4[1])
    third = swap(first, "yl", PAIR)
    fac = fac + swap(fac, "z", RING8_LAST[0])
    fac, outer, seen = tie((fac, outer, seen))
    outer = join(outer, seen, 100 * 10**8)
    seen = swap(outer, "z", RING8[1])
    fac = fac + swap(fac, "z", RING8_LAST[1])
    fac = fac + swap(fac, "z", RING8_LAST[2])
    fac, outer, seen, second, third = tie((fac, outer, seen, second, third))
    outer = join(outer, seen, 100 * 10**8)
    seen = swap(outer, "z", RING8[2])
    fourth = swap(second, "yl", PAIR)
    fac = fac + swap(fac, "x", RING4[0])
    fac = fac + swap(fac, "x", RING4[1])
    tokens = acts.shape[1] * lax.axis_size(("yl", "x", "z"))
    inverses = invert(fac, tokens)
    inverses, outer, seen = tie((inverses, outer, seen))
    parts = finish(layout, inverses, outer, seen, (first, second, third, fourth))
    parts = lax.all_to_all(parts, ("z", "yh", "core"), 0, 0, tiled=True)
    return collect(parts, groups).T


def solution(mesh):
    split = Mesh(mesh.devices.reshape(2, 4, 8, 2, 2), ("yl", "x", "z", "yh", "core"))
    dp, grp = ("yl", "x", "z"), ("yh", "core")
    return jax.shard_map(
        per_device,
        mesh=split,
        in_specs=(
            P(grp, dp, None),
            P(grp, dp, None),
            P(grp, None, None),
            P(grp, None, None),
            P(grp, dp, None),
        ),
        out_specs=P(grp, dp),
        check_vma=False,
    )
```

```python
import functools
import math

import jax
import jax.numpy as jnp
import numpy as np
from jax import lax
from jax.experimental import pallas as pl
from jax.experimental.pallas import tpu as pltpu
from jax.sharding import Mesh, PartitionSpec as P

SEQ = 64
DAMPING = 0.1
HIGH = lax.Precision.HIGHEST
F32 = jnp.float32
BF16 = jnp.bfloat16

PAIR = [(0, 1)]
RING4 = [[(0, 1), (2, 3)], [(1, 2), (3, 0)]]
RING8 = [
    [(0, 5), (1, 4), (2, 7), (3, 6)],
    [(0, 1), (2, 3), (4, 5), (6, 7)],
    [(1, 2), (3, 4), (5, 6), (7, 0)],
]

RING8_LAST = [RING8[1], RING8[2], [(1, 6), (2, 5), (0, 3), (7, 4)]]


def swap(value, axis, pairs):
    return lax.ppermute(value, axis, pairs + [(b, a) for a, b in pairs])


def gathered(rings, size):
    held = [[z] for z in range(size)]
    for pairs in rings:
        partner = {}
        for a, b in pairs:
            partner[a], partner[b] = b, a
        held = [held[z] + held[partner[z]] for z in range(size)]
    return held


def join_kernel(a, b, out):
    rows = a.shape[0]
    out[:rows, :] = a[...]
    out[rows:, :] = b[...]


def join(a, b, work):
    return pl.pallas_call(
        join_kernel,
        out_shape=jax.ShapeDtypeStruct((2 * a.shape[0], a.shape[1]), a.dtype),
        compiler_params=pltpu.CompilerParams(vmem_limit_bytes=4 * 2**20),
        cost_estimate=pl.CostEstimate(flops=work, bytes_accessed=2**20, transcendentals=0),
        name="join",
    )(a, b)


def layouts():
    trains, pairs = gathered(RING8, 8), gathered(RING4, 4)
    table = np.zeros((2, 4, 8, 16), np.int32)
    for y, x, z in np.ndindex(2, 4, 8):
        at = pairs[x]
        groups = [(y ^ i) * 2 + at[2 * j] // 2 for i in range(2) for j in range(2)]
        table[y, x, z, :14] = trains[z] + groups + [at[0] % 2, at[2] % 2]
    return table


def project_kernel(
    acts, grads, tab_in, tab_out, fac, outer, acts_v, grads_v, in_v, out_v, sems, *, scale, chunk
):
    tokens, width = acts.shape
    rank = tab_in.shape[0]
    cuts = [(slice(None), pl.ds(at, chunk)) for at in range(0, width, chunk)]
    arrays = ((tab_in, in_v), (tab_out, out_v), (acts, acts_v), (grads, grads_v))
    loads = [
        [
            pltpu.make_async_copy(source.at[cut], target.at[cut], sems.at[4 * i + j])
            for j, (source, target) in enumerate(arrays)
        ]
        for i, cut in enumerate(cuts)
    ]
    for load in loads:
        for copy in load:
            copy.start()

    def part(values, table, cut):
        matrix = ((2 * table[cut] - 1).astype(F32) * scale).astype(BF16)
        return lax.dot_general(
            values[cut], matrix, (((1,), (1,)), ((), ())), preferred_element_type=F32
        )

    x = g = jnp.zeros((tokens, rank), F32)
    for load, cut in zip(loads, cuts):
        for copy in load:
            copy.wait()
        x = x + part(acts_v, in_v, cut)
        g = g + part(grads_v, out_v, cut)
    both = jnp.concatenate([x, g], axis=1)
    left = lax.broadcasted_iota(jnp.int32, (rank, 2 * rank), 1) < rank
    total = jnp.zeros((rank, 2 * rank), F32)
    blocks = []
    for e in range(tokens // SEQ):
        rows = both[e * SEQ : (e + 1) * SEQ]
        gram = lax.dot_general(
            rows, rows, (((0,), (0,)), ((), ())), precision=HIGH, preferred_element_type=F32
        )
        total = total + jnp.where(left, gram[:rank], gram[rank:])
        blocks.append(gram[rank:, :rank])
    fac[...] = total
    outer[...] = jnp.concatenate(blocks, axis=1).astype(BF16)


def project(acts, grads, tab_in, tab_out):
    tokens, width = acts.shape
    rank = tab_in.shape[0]
    chunk = 256
    return pl.pallas_call(
        functools.partial(project_kernel, scale=1.0 / math.sqrt(width), chunk=chunk),
        in_specs=[pl.BlockSpec(memory_space=pl.ANY)] * 4,
        out_specs=[pl.BlockSpec(memory_space=pltpu.VMEM)] * 2,
        out_shape=[
            jax.ShapeDtypeStruct((rank, 2 * rank), F32),
            jax.ShapeDtypeStruct((rank, tokens // SEQ * rank), BF16),
        ],
        scratch_shapes=[
            pltpu.VMEM((tokens, width), BF16),
            pltpu.VMEM((tokens, width), BF16),
            pltpu.VMEM((rank, width), jnp.int32),
            pltpu.VMEM((rank, width), jnp.int32),
            pltpu.SemaphoreType.DMA((4 * width // chunk,)),
        ],
        compiler_params=pltpu.CompilerParams(vmem_limit_bytes=53 * 2**20 + 2**18),
        cost_estimate=pl.CostEstimate(
            flops=4 * tokens * width * rank, bytes_accessed=10 * 2**20, transcendentals=0
        ),
        name="project",
    )(acts, grads, tab_in, tab_out)


def solve_two(a, b, c, d, top, bottom):
    inv = 1.0 / (a * d - b * c)
    return (d * top - b * bottom) * inv, (a * bottom - c * top) * inv


def invert_pair(mat):
    rank = mat.shape[0]
    lane = lax.broadcasted_iota(jnp.int32, (1, 2 * rank), 1)
    row = lax.broadcasted_iota(jnp.int32, (rank, 1), 0)
    left = lane < rank
    place = lane & (rank - 1)
    for k in range(0, rank, 4):
        cols = [
            jnp.where(left, mat[:, k + i : k + i + 1], mat[:, rank + k + i : rank + k + i + 1])
            for i in range(4)
        ]
        m = [[cols[j][k + i : k + i + 1] for j in range(4)] for i in range(4)]
        rows = []
        for i in range(4):
            line = mat[k + i : k + i + 1]
            for j in range(4):
                line = jnp.where(place == k + j, 1.0 if i == j else 0.0, line)
            rows.append(line)
        head = m[0][0], m[0][1], m[1][0], m[1][1]
        u0, u1 = solve_two(*head, rows[0], rows[1])
        p0, p1 = solve_two(*head, m[0][2], m[1][2])
        q0, q1 = solve_two(*head, m[0][3], m[1][3])
        schur = (
            m[2][2] - m[2][0] * p0 - m[2][1] * p1,
            m[2][3] - m[2][0] * q0 - m[2][1] * q1,
            m[3][2] - m[3][0] * p0 - m[3][1] * p1,
            m[3][3] - m[3][0] * q0 - m[3][1] * q1,
        )
        t0 = rows[2] - m[2][0] * u0 - m[2][1] * u1
        t1 = rows[3] - m[3][0] * u0 - m[3][1] * u1
        v0, v1 = solve_two(*schur, t0, t1)
        solved = [u0 - p0 * v0 - q0 * v1, u1 - p1 * v0 - q1 * v1, v0, v1]
        rest = jnp.where((place >= k) & (place < k + 4), 0.0, mat)
        for i in range(4):
            rest = rest - cols[i] * solved[i]
        for i in range(4):
            rest = jnp.where(row == k + i, solved[i], rest)
        mat = rest
    return mat


def halves(value):
    hi = value.astype(BF16)
    return hi, (value - hi.astype(F32)).astype(BF16)


def invert_kernel(fac, out, *, tokens):
    rank = fac.shape[0]
    mat = fac[...] / tokens
    lane = lax.broadcasted_iota(jnp.int32, (rank, 2 * rank), 1)
    row = lax.broadcasted_iota(jnp.int32, (rank, 2 * rank), 0)
    left = lane < rank
    diag = jnp.where((lane & (rank - 1)) == row, mat, 0.0)
    ridge_in = DAMPING * jnp.sum(jnp.where(left, diag, 0.0), keepdims=True) / rank
    ridge_out = DAMPING * jnp.sum(jnp.where(left, 0.0, diag), keepdims=True) / rank
    ridge = jnp.where(left, ridge_in, ridge_out)
    out[...] = invert_pair(mat + jnp.where((lane & (rank - 1)) == row, ridge, 0.0))


def invert(fac, tokens):
    return pl.pallas_call(
        functools.partial(invert_kernel, tokens=tokens),
        out_shape=jax.ShapeDtypeStruct(fac.shape, F32),
        compiler_params=pltpu.CompilerParams(vmem_limit_bytes=4 * 2**20),
        cost_estimate=pl.CostEstimate(
            flops=25 * 10**8, bytes_accessed=2**16, transcendentals=0
        ),
        name="invert",
    )(fac)


def finish_kernel(layout, inverses, near, far, *refs):
    queries, (out, held, train, scores, parts_v) = refs[:4], refs[4:]
    rank = inverses.shape[0]
    mat = inverses[...]
    inv_in = mat[:, :rank]
    inv_out = mat[:, rank:]
    out_hi, out_lo = halves(inv_out)
    four = 4 * rank
    rows4 = lax.broadcasted_iota(jnp.int32, (four, four), 0) // rank
    cols4 = lax.broadcasted_iota(jnp.int32, (four, four), 1) // rank
    tiled = jnp.concatenate([inv_in] * 4, axis=1)
    tiled = jnp.concatenate([tiled] * 4, axis=0)
    in_hi, in_lo = halves(jnp.where(rows4 == cols4, tiled, 0.0))
    dot = functools.partial(jnp.dot, preferred_element_type=F32)
    half = near.shape[0] // rank
    places = 2 * half
    wide = near.shape[1]
    out_both = jnp.concatenate([out_hi, out_lo], axis=0)
    for p in range(places):
        at = p % half * rank
        both = dot(out_both, (near if p < half else far)[at : at + rank, :])
        hi, lo = halves(both[:rank] + both[rank:])
        parts_v[p * rank : (p + 1) * rank, :] = hi
        parts_v[(places + p) * rank : (places + p + 1) * rank, :] = lo
    for c in range(wide // four):
        cut = slice(c * four, (c + 1) * four)
        main = dot(parts_v[:, cut], in_hi)
        rest = dot(parts_v[: places * rank, cut], in_lo)
        second = main[: places * rank] + (rest + main[places * rank :])
        held[:, :, cut] = second.reshape(places, rank, four)
    low = lax.broadcasted_iota(jnp.int32, (places, 2 * rank), 1) < rank
    for o in range(0, rank, 2):
        even = held[:, o, :]
        odd = held[:, o + 1, :]
        pieces = []
        for pair in range(wide // (2 * rank)):
            cut = slice(pair * 2 * rank, (pair + 1) * 2 * rank)
            a, b = even[:, cut], odd[:, cut]
            pieces.append(jnp.where(low, a, pltpu.roll(b, rank, 1)))
            pieces.append(jnp.where(low, pltpu.roll(a, rank, 1), b))
        train[:, o * rank : (o + 2) * rank] = jnp.concatenate(pieces, axis=0).astype(BF16)
    nt = (((1,), (1,)), ((), ()))
    for i in range(2):
        parts = [
            lax.dot_general(train[...], block[...], nt, preferred_element_type=F32)
            for block in queries[2 * i : 2 * i + 2]
        ]
        scores[i] = jnp.concatenate(parts, axis=1)
    examples = wide // rank
    rows_out = examples // 2
    run = scores.shape[2] // 4
    for p in range(places):
        for i in range(2):
            rows = scores[i, pl.ds(p, examples, places), :]
            for j in range(2):
                pair = rows[:, 2 * j * run : 2 * (j + 1) * run]
                turned = jnp.concatenate([pair[:, run:], pair[:, :run]], axis=1)
                cut = jnp.where(layout[places + 4 + j] == 1, turned, pair)
                target = layout[p] * 4 + layout[places + 2 * i + j]
                out[target] = jnp.concatenate([cut[:rows_out], cut[rows_out:]], axis=1)


def finish(layout, inverses, near, far, queries):
    rank = inverses.shape[0]
    places = 2 * near.shape[0] // rank
    examples = near.shape[1] // rank
    count = queries[0].shape[0]
    return pl.pallas_call(
        finish_kernel,
        out_shape=jax.ShapeDtypeStruct((places * 4, examples // 2, 2 * count), F32),
        in_specs=[pl.BlockSpec(memory_space=pltpu.SMEM)]
        + [pl.BlockSpec(memory_space=pltpu.VMEM)] * 7,
        scratch_shapes=[
            pltpu.VMEM((places, rank, near.shape[1]), F32),
            pltpu.VMEM((places * examples, rank * rank), BF16),
            pltpu.VMEM((2, places * examples, 2 * count), F32),
            pltpu.VMEM((2 * places * rank, near.shape[1]), BF16),
        ],
        compiler_params=pltpu.CompilerParams(vmem_limit_bytes=16 * 2**20),
        cost_estimate=pl.CostEstimate(
            flops=40 * 10**8, bytes_accessed=2**20, transcendentals=0
        ),
        name="finish",
    )(layout, inverses, near, far, *queries)


def collect_kernel(parts, out, *, groups):
    places = parts.shape[0] // groups
    half, wide = parts.shape[1], parts.shape[2] // 2
    runs = wide // 2
    tops, bottoms = [], []
    for p in range(places):
        total = parts[p * groups]
        for g in range(1, groups):
            total = total + parts[p * groups + g]
        tops.append(total[:, :wide])
        bottoms.append(total[:, wide:])
    for rows, cuts in ((0, tops), (half, bottoms)):
        line = [cut[:, r * runs : (r + 1) * runs] for r in range(2) for cut in cuts]
        out[rows : rows + half, :] = jnp.concatenate(line, axis=1)


def collect(parts, groups):
    places = parts.shape[0] // groups
    return pl.pallas_call(
        functools.partial(collect_kernel, groups=groups),
        out_shape=jax.ShapeDtypeStruct(
            (2 * parts.shape[1], places * parts.shape[2] // 2), F32
        ),
        compiler_params=pltpu.CompilerParams(vmem_limit_bytes=4 * 2**20),
        name="collect",
    )(parts)


def per_device(acts, out_grads, proj_in, proj_out, query_grads):
    groups = lax.axis_size(("yh", "core"))
    tie = lax.optimization_barrier
    own = query_grads[0]
    got = swap(own, "x", RING4[0])
    layout = jnp.asarray(layouts())[
        lax.axis_index("yl"), lax.axis_index("x"), lax.axis_index("z")
    ]
    fac, outer = project(acts[0], out_grads[0], proj_in[0], proj_out[0])
    seen = swap(outer, "z", RING8[0])
    fac = fac + swap(fac, "yl", PAIR)
    fac, own, got = tie((fac, own, got))
    first = join(own, got, 1 * 10**8)
    second = swap(first, "x", RING4[1])
    third = swap(first, "yl", PAIR)
    fac = fac + swap(fac, "z", RING8_LAST[0])
    fac, outer, seen = tie((fac, outer, seen))
    outer = join(outer, seen, 100 * 10**8)
    seen = swap(outer, "z", RING8[1])
    fac = fac + swap(fac, "z", RING8_LAST[1])
    fac = fac + swap(fac, "z", RING8_LAST[2])
    fac, outer, seen, second, third = tie((fac, outer, seen, second, third))
    outer = join(outer, seen, 100 * 10**8)
    seen = swap(outer, "z", RING8[2])
    fourth = swap(second, "yl", PAIR)
    fac = fac + swap(fac, "x", RING4[0])
    fac = fac + swap(fac, "x", RING4[1])
    tokens = acts.shape[1] * lax.axis_size(("yl", "x", "z"))
    inverses = invert(fac, tokens)
    inverses, outer, seen = tie((inverses, outer, seen))
    parts = finish(layout, inverses, outer, seen, (first, second, third, fourth))
    parts = lax.all_to_all(parts, ("z", "yh", "core"), 0, 0, tiled=True)
    return collect(parts, groups).T


def solution(mesh):
    split = Mesh(mesh.devices.reshape(2, 4, 8, 2, 2), ("yl", "x", "z", "yh", "core"))
    dp, grp = ("yl", "x", "z"), ("yh", "core")
    return jax.shard_map(
        per_device,
        mesh=split,
        in_specs=(
            P(grp, dp, None),
            P(grp, dp, None),
            P(grp, None, None),
            P(grp, None, None),
            P(grp, dp, None),
        ),
        out_specs=P(grp, dp),
        check_vma=False,
    )
```
